256 devices in a mesh: frame: 64 (over x_lo, y, z), space: 4 (over x_hi, core).
Axes of the slice: x: 4 (x_hi: 2, x_lo: 2; x = x_hi * 2 + x_lo), y: 4, z: 8, core: 2. Of those that a mesh axis runs over, the one named last changes fastest.
Arguments:
- latent: bfloat16 [64, 48, 48, 640], P('frame', 'space'), may hold values from -41 to 41
- reference_states: bfloat16 [48, 48, 640], P('space'), may hold values from -6 to 6
- group_gain: float32 [640], replicated, may hold values from 0.1 to 1.9
- conv_weight: bfloat16 [3, 3, 640, 640], replicated, may hold values from -0.078125 to 0.078125
- norm_gain: float32 [640], replicated, may hold values from 0.1 to 1.9
- spatial_query: bfloat16 [640, 320], replicated, may hold values from -0.75 to 0.75
- spatial_key: bfloat16 [640, 320], replicated, may hold values from -0.25 to 0.25
- spatial_value: bfloat16 [640, 320], replicated, may hold values from -0.25 to 0.25
- spatial_out: bfloat16 [320, 640], replicated, may hold values from -0.3125 to 0.3125
- frame_gain: float32 [640], replicated, may hold values from 0.1 to 1.9
- temporal_query: bfloat16 [640, 320], replicated, may hold values from -0.75 to 0.75
- temporal_key: bfloat16 [640, 320], replicated, may hold values from -0.25 to 0.25
- temporal_value: bfloat16 [640, 320], replicated, may hold values from -0.25 to 0.25
- temporal_out: bfloat16 [320, 640], replicated, may hold values from -0.3125 to 0.3125
Outputs:
- output: bfloat16 [64, 48, 48, 640], P('frame', 'space')
The draws below stay inside these ranges and needn't reach their ends.
All inputs are finite; a program needn't handle non-finite values.
Results may differ from the reference program's by a relative error of at most 0.018.
Values may be sent and summed in bfloat16 or wider, within the bound.
No kernel may reach another device: no remote copies, remote signals or barrier semaphores. Data moves between devices by JAX's collectives and lax.ppermute only.
A program may use at most 128 MiB of HBM per device.

```python
import jax
import jax.numpy as jnp
from jax import lax

C = 640
HEADS = 4
HEAD_DIM = 80
INNER = 320
GROUPS = 32
W = 48
H = 48
FRAMES = 64


def draw_latent(key, part):
    key = jax.random.fold_in(key, 11)
    key_base, key_chan, key_frame = jax.random.split(key, 3)
    heights = jnp.arange(H, dtype=jnp.float32) / (H - 1)
    base = jnp.clip(jax.random.normal(key_base, (FRAMES, H, W, C), jnp.float32), -4.0, 4.0)
    row_scale = 0.35 * jnp.power(10.0, heights)
    chan_scale = jnp.exp(jax.random.uniform(key_chan, (C,), jnp.float32, -0.7, 0.7))
    frame_scale = jnp.exp(jax.random.uniform(key_frame, (FRAMES,), jnp.float32, -0.35, 0.35))
    return (base * row_scale[None, :, None, None] * chan_scale * frame_scale[:, None, None, None]).astype(jnp.bfloat16)


def level_of(own_key, shape, shards, low, largest):
    loudness = 1.0
    for axis_at, shards_of in shards:
        draws = jax.random.uniform(jax.random.fold_in(jax.random.fold_in(own_key, 6), axis_at), (shards_of,), jnp.float32, low / len(shards), largest / len(shards))
        loudness = loudness * jnp.repeat(jnp.exp(draws), shape[axis_at] // shards_of).reshape((-1,) + (1,) * (len(shape) - 1 - axis_at))
    return loudness


def normal_values(stream_key, dims, deviation, most, shards=(), kind=jnp.bfloat16):
    entries = jax.random.normal(stream_key, dims, jnp.float32) * deviation
    if len(shards) > 0:
        entries = level_of(stream_key, dims, shards, -0.22, 0.18) * entries
    return jnp.clip(entries, min=-most, max=most).astype(kind)


def setup_inputs(seed: int = 0) -> dict:
    seeds = jax.random.split(jax.random.key(seed), 15)
    latent = draw_latent(jax.random.fold_in(seeds[14], 71), 0)
    reference_states = normal_values(seeds[1], (H, W, C), 1.0, 6.0, ((0, 4),))
    group_gain = jnp.clip(1.0 + 0.18 * jax.random.normal(seeds[2], (C,), jnp.float32), 0.1, 1.9)
    conv_weight = normal_values(seeds[3], (3, 3, C, C), (9 * C) ** -0.5, 0.078125)
    norm_gain = jnp.clip(1.0 + 0.18 * jax.random.normal(seeds[4], (C,), jnp.float32), 0.1, 1.9)
    spatial_query = normal_values(seeds[5], (C, INNER), (C // 9) ** -0.5, 0.75)
    spatial_key = normal_values(seeds[6], (C, INNER), C ** -0.5, 0.25)
    spatial_value = normal_values(seeds[7], (C, INNER), C ** -0.5, 0.25)
    spatial_out = normal_values(seeds[8], (INNER, C), INNER ** -0.5, 0.3125)
    frame_gain = jnp.clip(1.0 + 0.18 * jax.random.normal(seeds[9], (C,), jnp.float32), 0.1, 1.9)
    temporal_query = normal_values(seeds[10], (C, INNER), (C // 9) ** -0.5, 0.75)
    temporal_key = normal_values(seeds[11], (C, INNER), C ** -0.5, 0.25)
    temporal_value = normal_values(seeds[12], (C, INNER), C ** -0.5, 0.25)
    temporal_out = normal_values(seeds[13], (INNER, C), INNER ** -0.5, 0.3125)
    return {"latent": latent, "reference_states": reference_states, "group_gain": group_gain, "conv_weight": conv_weight, "norm_gain": norm_gain, "spatial_query": spatial_query, "spatial_key": spatial_key, "spatial_value": spatial_value, "spatial_out": spatial_out, "frame_gain": frame_gain, "temporal_query": temporal_query, "temporal_key": temporal_key, "temporal_value": temporal_value, "temporal_out": temporal_out}


epsilon = 1e-05

def layer_norm(values, factor):
    centre = lax.optimization_barrier(jnp.mean(values, axis=-1, keepdims=True))
    spread = lax.optimization_barrier(jnp.mean(jnp.square(values - centre), axis=-1, keepdims=True))
    return (values - centre) * lax.rsqrt(spread + epsilon) * factor

def rounded(values):
    return lax.optimization_barrier(values.astype(jnp.bfloat16))

def spatial_attention(queries, keys_all, values_all):
    query_heads = queries.astype(jnp.float32).reshape(queries.shape[0], HEADS, HEAD_DIM)
    key_heads = keys_all.astype(jnp.float32).reshape(keys_all.shape[0], HEADS, HEAD_DIM)
    value_heads = values_all.astype(jnp.float32).reshape(values_all.shape[0], HEADS, HEAD_DIM)
    scores = jnp.einsum('qhd,khd->hqk', query_heads, key_heads, precision=lax.Precision.HIGHEST) * HEAD_DIM ** (-0.5)
    exps = jnp.exp(scores)
    totals = lax.optimization_barrier(jnp.sum(exps, axis=-1))
    probs = rounded(exps).astype(jnp.float32)
    weighted = jnp.einsum('hqk,khd->qhd', probs, value_heads, precision=lax.Precision.HIGHEST)
    attended = weighted / jnp.transpose(totals)[:, :, None]
    return attended.astype(jnp.bfloat16).reshape(queries.shape[0], INNER)

def reference(latent, reference_states, group_gain, conv_weight, norm_gain, spatial_query, spatial_key, spatial_value, spatial_out, frame_gain, temporal_query, temporal_key, temporal_value, temporal_out):
    per_group = C // GROUPS
    members = H * W * per_group
    wide = latent.astype(jnp.float32)
    grouped = wide.reshape(FRAMES, H * W, GROUPS, per_group)
    group_sum = lax.optimization_barrier(jnp.sum(grouped, axis=(1, 3)))
    group_sq = lax.optimization_barrier(jnp.sum(grouped * grouped, axis=(1, 3)))
    average = group_sum / members
    variance = group_sq / members - average * average
    scaling = lax.rsqrt(variance + epsilon)
    average_c = jnp.repeat(average, per_group, axis=1)[:, None, None, :]
    scaling_c = jnp.repeat(scaling, per_group, axis=1)[:, None, None, :]
    activated = jax.nn.silu((wide - average_c) * scaling_c * group_gain).astype(jnp.bfloat16)
    kernel = conv_weight.astype(jnp.float32)

    def convolve(pair):
        frame_act, frame_lat = pair
        result = lax.conv_general_dilated(frame_act.astype(jnp.float32)[None], kernel, (1, 1), ((1, 1), (1, 1)), dimension_numbers=('NHWC', 'HWIO', 'NHWC'), precision=lax.Precision.HIGHEST)[0]
        return (frame_lat.astype(jnp.float32) + result).astype(jnp.bfloat16)
    hidden = lax.map(convolve, (activated, latent))
    ref_normed = layer_norm(reference_states.astype(jnp.float32).reshape(H * W, C), 1.0).astype(jnp.bfloat16)
    ref_key = rounded(jnp.dot(ref_normed, spatial_key, preferred_element_type=jnp.float32))
    ref_value = rounded(jnp.dot(ref_normed, spatial_value, preferred_element_type=jnp.float32))

    def spatial(frame_hidden):
        tokens = frame_hidden.reshape(H * W, C)
        normed = layer_norm(tokens.astype(jnp.float32), norm_gain).astype(jnp.bfloat16)
        queries = rounded(jnp.dot(normed, spatial_query, preferred_element_type=jnp.float32))
        own_keys = rounded(jnp.dot(normed, spatial_key, preferred_element_type=jnp.float32))
        own_values = rounded(jnp.dot(normed, spatial_value, preferred_element_type=jnp.float32))
        keys_all = jnp.concatenate([own_keys, ref_key], axis=0)
        values_all = jnp.concatenate([own_values, ref_value], axis=0)
        attended = spatial_attention(queries, keys_all, values_all)
        update = jnp.dot(attended, spatial_out, preferred_element_type=jnp.float32)
        return (tokens.astype(jnp.float32) + update).astype(jnp.bfloat16)
    mixed = lax.map(spatial, hidden)
    framed = layer_norm(mixed.astype(jnp.float32), frame_gain).astype(jnp.bfloat16)
    t_query = rounded(jnp.dot(framed, temporal_query, preferred_element_type=jnp.float32))
    t_key = rounded(jnp.dot(framed, temporal_key, preferred_element_type=jnp.float32))
    t_value = rounded(jnp.dot(framed, temporal_value, preferred_element_type=jnp.float32))
    query_heads = t_query.astype(jnp.float32).reshape(FRAMES, H * W, HEADS, HEAD_DIM)
    key_heads = t_key.astype(jnp.float32).reshape(FRAMES, H * W, HEADS, HEAD_DIM)
    value_heads = t_value.astype(jnp.float32).reshape(FRAMES, H * W, HEADS, HEAD_DIM)
    scores = jnp.einsum('qphd,kphd->phqk', query_heads, key_heads, precision=lax.Precision.HIGHEST) * HEAD_DIM ** (-0.5)
    exps = jnp.exp(scores)
    totals = lax.optimization_barrier(jnp.sum(exps, axis=-1))
    probs = rounded(exps).astype(jnp.float32)
    weighted = jnp.einsum('phqk,kphd->qphd', probs, value_heads, precision=lax.Precision.HIGHEST)
    t_attended = (weighted / jnp.transpose(totals, (2, 0, 1))[..., None]).astype(jnp.bfloat16).reshape(FRAMES, H * W, INNER)
    update = jnp.dot(t_attended, temporal_out, preferred_element_type=jnp.float32)
    output = (mixed.astype(jnp.float32) + update).astype(jnp.bfloat16)
    return output.reshape(FRAMES, H, W, C)
```

```python
import functools

import jax
import jax.numpy as jnp
from jax import lax
from jax.experimental import pallas as pl
from jax.experimental.pallas import tpu as pltpu
from jax.sharding import PartitionSpec as P

HEADS = 4
HEAD_DIM = 80
GROUPS = 32
INNER = 320
C = 640
W = 48
STRIP = 12
CELLS = STRIP * W
FRAMES = 64
PLACES = CELLS // FRAMES
LANES = 128
SENT = 48
BACK = 24

epsilon = 1e-05
QUERY_SCALE = HEAD_DIM**-0.5 * 1.4426950408889634

KEY_WINDOW = ((0, 128), (0, 256), (128, 256), (128, 384))
VALUE_WINDOW = ((256, 512), (384, 512), (384, 640), (512, 640))
ACC_AT = (0, 256, 384, 640)
ACC_WIDTH = 768

f32 = jnp.float32
bf16 = jnp.bfloat16


def lane_iota(width, start=0):
    return lax.broadcasted_iota(jnp.int32, (1, width), 1) + start


def layer_norm(values, factor):
    centre = jnp.mean(values, axis=-1, keepdims=True)
    shifted = values - centre
    spread = jnp.mean(shifted * shifted, axis=-1, keepdims=True)
    normed = shifted * lax.rsqrt(spread + epsilon)
    return normed if factor is None else normed * factor


def dot(a, b):
    return jnp.dot(a, b, preferred_element_type=f32)


def vmem(count):
    return [pl.BlockSpec(memory_space=pltpu.VMEM)] * count


def call(body, outs, operands, scratch=(), flops=0, smem=0, limit=48):
    single = not isinstance(outs, (list, tuple))
    specs = [pl.BlockSpec(memory_space=pltpu.SMEM)] * smem + vmem(len(operands) - smem)
    return pl.pallas_call(
        body,
        out_shape=outs,
        in_specs=specs,
        out_specs=vmem(1)[0] if single else vmem(len(outs)),
        scratch_shapes=list(scratch),
        compiler_params=pltpu.CompilerParams(vmem_limit_bytes=limit * 1024 * 1024),
        cost_estimate=pl.CostEstimate(flops=flops, bytes_accessed=1 << 20, transcendentals=0),
    )(*operands)


def stats_kernel(x_ref, sums_ref, top_ref, bottom_ref):
    total = jnp.zeros((1, C), f32)
    square = jnp.zeros((1, C), f32)
    for r in range(STRIP):
        v = x_ref[r * W : (r + 1) * W, :].astype(f32)
        total = total + jnp.sum(v, axis=0, keepdims=True)
        square = square + jnp.sum(v * v, axis=0, keepdims=True)
    pieces = []
    for v in (total, square):
        high = v.astype(bf16).astype(f32)
        middle = (v - high).astype(bf16).astype(f32)
        pieces += [high, middle, v - high - middle]
    pieces += [jnp.zeros((1, C), f32)] * 2
    row = lax.broadcasted_iota(jnp.int32, (8, C), 0)
    stacked = jnp.zeros((8, C), f32)
    for i, p in enumerate(pieces):
        stacked = jnp.where(row == i, p, stacked)
    per = C // GROUPS
    column_group = jnp.floor((lane_iota(C).astype(f32) + 0.5) * (1.0 / per))
    row_at = lax.broadcasted_iota(jnp.int32, (C, 1), 0).astype(f32)
    row_group = jnp.floor((row_at + 0.5) * (1.0 / per))
    same = jnp.where(row_group == column_group, 1.0, 0.0).astype(bf16)
    grouped = dot(stacked.astype(bf16), same)
    group_sum = grouped[0:1] + grouped[1:2] + grouped[2:3]
    group_sq = grouped[3:4] + grouped[4:5] + grouped[5:6]
    sums_ref[...] = jnp.where(row == 0, group_sum, jnp.where(row == 1, group_sq, 0.0))
    top_ref[...] = x_ref[0:W, :]
    bottom_ref[...] = x_ref[CELLS - W :, :]


def reference_kernel(states_ref, weight_ref, out_ref):
    normed = layer_norm(states_ref[...].astype(f32), None).astype(bf16)
    out_ref[...] = dot(normed, weight_ref[...]).astype(bf16)


def conv_kernel(
    flags_ref,
    s0_ref,
    s1_ref,
    s2_ref,
    s3_ref,
    x_ref,
    above_ref,
    below_ref,
    gain_ref,
    kernel_ref,
    norm_gain_ref,
    query_ref,
    kv_ref,
    hidden_out,
    query_out,
    kv_out,
    lhs,
):
    sums = (s0_ref[...] + s1_ref[...]) + (s2_ref[...] + s3_ref[...])
    members = float(4 * CELLS * (C // GROUPS))
    average = sums[0:1] / members
    variance = sums[1:2] / members - average * average
    factor = lax.rsqrt(variance + epsilon) * gain_ref[...]
    at = lax.broadcasted_iota(jnp.int32, (W, 1), 0)

    def place(r, block, keep):
        v = (block.astype(f32) - average) * factor
        act = (0.5 * v) * (1.0 + jnp.tanh(0.5 * v))
        if keep is not None:
            act = jnp.where(keep > 0.5, act, 0.0)
        rows = slice(r * W, (r + 1) * W)
        lhs[rows, C : 2 * C] = act.astype(bf16)
        lhs[rows, 0:C] = jnp.where(at == 0, 0.0, pltpu.roll(act, 1, 0)).astype(bf16)
        lhs[rows, 2 * C :] = jnp.where(at == W - 1, 0.0, pltpu.roll(act, W - 1, 0)).astype(bf16)

    place(0, above_ref[...], flags_ref[0, 0])
    for r in range(STRIP):
        place(r + 1, x_ref[r * W : (r + 1) * W, :], None)
    place(STRIP + 1, below_ref[...], flags_ref[0, 1])
    total = dot(lhs[0:CELLS, :], kernel_ref[0])
    total = total + dot(lhs[W : W + CELLS, :], kernel_ref[1])
    total = total + dot(lhs[2 * W : 2 * W + CELLS, :], kernel_ref[2])
    hidden = (x_ref[...].astype(f32) + total).astype(bf16)
    hidden_out[...] = hidden
    normed = layer_norm(hidden.astype(f32), norm_gain_ref[...]).astype(bf16)
    query_out[...] = (dot(normed, query_ref[...]) * QUERY_SCALE).astype(bf16)
    kv_out[...] = dot(normed, kv_ref[...]).astype(bf16)


def head_query(query, h):
    low, high = KEY_WINDOW[h]
    lane = lane_iota(high - low, low)
    inside = (lane >= h * HEAD_DIM) & (lane < (h + 1) * HEAD_DIM)
    return jnp.where(inside, query[:, low:high], jnp.zeros((), bf16))


def inside_value(h):
    low, high = VALUE_WINDOW[h]
    lane = lane_iota(high - low, low)
    return (lane >= INNER + h * HEAD_DIM) & (lane < INNER + (h + 1) * HEAD_DIM)


def attend(query, kv_refs, tile, start):
    gathered = []
    for h in range(HEADS):
        key_low, key_high = KEY_WINDOW[h]
        low, high = VALUE_WINDOW[h]
        mine = head_query(query, h)
        inside = inside_value(h)
        acc = None if start is None else start(h)
        for ref in kv_refs:
            for first in range(0, ref.shape[0], tile):
                rows = slice(first, min(first + tile, ref.shape[0]))
                scores = lax.dot_general(
                    mine,
                    ref[rows, key_low:key_high],
                    (((1,), (1,)), ((), ())),
                    preferred_element_type=f32,
                )
                weights = jnp.exp2(scores).astype(bf16)
                values = jnp.where(inside, ref[rows, low:high], jnp.ones((), bf16))
                part = dot(weights, values)
                acc = part if acc is None else acc + part
        gathered.append(acc)
    return gathered


def normalised(gathered):
    blocks = [None, None, None]
    for h in range(HEADS):
        low, high = VALUE_WINDOW[h]
        acc = gathered[h]
        spare = 0 if INNER + h * HEAD_DIM > low else high - low - 1
        result = acc * (1.0 / acc[:, spare : spare + 1])
        result = jnp.where(inside_value(h), result, 0.0)
        for b in range((high - low) // LANES):
            at = low // LANES + b - 2
            piece = result[:, b * LANES : (b + 1) * LANES]
            blocks[at] = piece if blocks[at] is None else blocks[at] + piece
    return blocks


def attention_kernel(n_kv, has_start, tile, *refs):
    query_ref = refs[0]
    kv_refs = refs[1 : 1 + n_kv]
    start = None
    if has_start:
        acc_ref = refs[1 + n_kv]
        start = lambda h: acc_ref[:, ACC_AT[h] : ACC_AT[h] + VALUE_WINDOW[h][1] - VALUE_WINDOW[h][0]]
    out_ref = refs[-1]
    for h, acc in enumerate(attend(query_ref[...], kv_refs, tile, start)):
        out_ref[:, ACC_AT[h] : ACC_AT[h] + acc.shape[1]] = acc


def last_attention_kernel(
    n_kv, tile, query_ref, acc_ref, hidden_ref, weight_ref, gain_ref, *refs
):
    kv_refs = refs[:n_kv]
    mixed_out, sent_out, rows = refs[n_kv:]
    start = lambda h: acc_ref[:, ACC_AT[h] : ACC_AT[h] + VALUE_WINDOW[h][1] - VALUE_WINDOW[h][0]]
    blocks = normalised(attend(query_ref[...], kv_refs, tile, start))
    update = None
    for b in range(3):
        part = dot(blocks[b].astype(bf16), weight_ref[b * LANES : (b + 1) * LANES, :])
        update = part if update is None else update + part
    mixed = (hidden_ref[...].astype(f32) + update).astype(bf16)
    mixed_out[...] = mixed
    framed = layer_norm(mixed.astype(f32), gain_ref[...])
    for j in range(PLACES):
        for c in range(C // LANES):
            rows[pl.ds(j * 5 + c, FRAMES, stride=SENT), :] = framed[
                j * FRAMES : (j + 1) * FRAMES, c * LANES : (c + 1) * LANES
            ]
    for r in range(PLACES * 5, SENT):
        rows[pl.ds(r, FRAMES, stride=SENT), :] = jnp.zeros((FRAMES, LANES), f32)
    sent_out[...] = rows[...].astype(bf16)


def temporal_kernel(got_ref, query_ref, kv_weight_ref, out_ref, rows, tokens, result):
    rows[...] = got_ref[...].astype(f32)
    for j in range(PLACES):
        for c in range(C // LANES):
            tokens[j * FRAMES : (j + 1) * FRAMES, c * LANES : (c + 1) * LANES] = rows[
                pl.ds(j * 5 + c, FRAMES, stride=SENT), :
            ].astype(bf16)
    query = (dot(tokens[...], query_ref[...]) * QUERY_SCALE).astype(bf16)
    kv = dot(tokens[...], kv_weight_ref[...]).astype(bf16)
    span = 3 * FRAMES
    row_place = lax.broadcasted_iota(jnp.int32, (span, span), 0) // FRAMES
    column_place = lax.broadcasted_iota(jnp.int32, (span, span), 1) // FRAMES
    same = row_place == column_place
    for first in range(0, CELLS, span):
        gathered = []
        for h in range(HEADS):
            key_low, key_high = KEY_WINDOW[h]
            low, high = VALUE_WINDOW[h]
            scores = lax.dot_general(
                head_query(query[first : first + span], h),
                kv[first : first + span, key_low:key_high],
                (((1,), (1,)), ((), ())),
                preferred_element_type=f32,
            )
            weights = jnp.where(same, jnp.exp2(scores), 0.0).astype(bf16)
            values = jnp.where(
                inside_value(h), kv[first : first + span, low:high], jnp.ones((), bf16)
            )
            gathered.append(dot(weights, values))
        blocks = normalised(gathered)
        for b in range(3):
            result[first : first + span, b * LANES : (b + 1) * LANES] = blocks[b]
    for j in range(PLACES):
        cell = slice(j * FRAMES, (j + 1) * FRAMES)
        for b in range(2):
            rows[pl.ds(j * 2 + b, FRAMES, stride=BACK), :] = result[
                cell, (1 + b) * LANES : (2 + b) * LANES
            ]
    for pair in range((PLACES + 1) // 2):
        half = result[2 * pair * FRAMES : (2 * pair + 1) * FRAMES, 0:LANES]
        if 2 * pair + 1 < PLACES:
            other = result[(2 * pair + 1) * FRAMES : (2 * pair + 2) * FRAMES, 0:LANES]
            half = half + pltpu.roll(other, LANES // 2, 1)
        rows[pl.ds(2 * PLACES + pair, FRAMES, stride=BACK), :] = half
    rows[pl.ds(BACK - 1, FRAMES, stride=BACK), :] = jnp.zeros((FRAMES, LANES), f32)
    out_ref[...] = rows[0 : FRAMES * BACK, :].astype(bf16)


def final_kernel(got_ref, weight_ref, mixed_ref, out_ref, rows, attended):
    rows[...] = got_ref[...].astype(f32)
    upper = lane_iota(LANES) >= LANES // 2
    for j in range(PLACES):
        cell = slice(j * FRAMES, (j + 1) * FRAMES)
        for b in range(2):
            attended[cell, (1 + b) * LANES : (2 + b) * LANES] = rows[
                pl.ds(j * 2 + b, FRAMES, stride=BACK), :
            ].astype(bf16)
        half = rows[pl.ds(2 * PLACES + j // 2, FRAMES, stride=BACK), :]
        if j % 2:
            half = pltpu.roll(half, LANES // 2, 1)
        attended[cell, 0:LANES] = jnp.where(upper, half, 0.0).astype(bf16)
    update = dot(attended[...], weight_ref[...])
    out_ref[...] = (mixed_ref[...].astype(f32) + update).astype(bf16)


def struct(shape, dtype):
    return jax.ShapeDtypeStruct(shape, dtype)


def on_device(
    latent,
    reference_states,
    group_gain,
    conv_weight,
    norm_gain,
    spatial_query,
    spatial_key,
    spatial_value,
    spatial_out,
    frame_gain,
    temporal_query,
    temporal_key,
    temporal_value,
    temporal_out,
):
    x = latent.reshape(CELLS, C)
    strip_at = lax.axis_index("space")
    flags = jnp.stack([strip_at > 0, strip_at < 3]).astype(f32).reshape(1, 2)

    def swap(value, k):
        return lax.ppermute(value, "space", [(i, i ^ k) for i in range(4)])

    pad_query = lambda w: jnp.pad(w, ((0, 0), (0, 64)))
    pad_out = lambda w: jnp.pad(w, ((64, 0), (0, 0)))
    spatial_kv = jnp.concatenate([spatial_key, spatial_value], axis=1)
    temporal_kv = jnp.concatenate([temporal_key, temporal_value], axis=1)

    sums, top, bottom = call(
        stats_kernel,
        [struct((8, C), f32), struct((W, C), bf16), struct((W, C), bf16)],
        [x],
    )
    others = [swap(sums, k) for k in (2, 3, 1)]
    above = lax.ppermute(bottom, "space", [(0, 1), (1, 2), (2, 3)])
    below = lax.ppermute(top, "space", [(1, 0), (2, 1), (3, 2)])

    ref_kv = call(
        reference_kernel,
        struct((CELLS, C), bf16),
        [reference_states.reshape(CELLS, C), spatial_kv],
        flops=2 * CELLS * C * C,
    )
    ref_far = swap(ref_kv, 2)
    ref_near = swap(ref_kv, 1)
    ref_far_near = swap(ref_far, 1)

    hidden, query, kv = call(
        conv_kernel,
        [struct((CELLS, C), bf16), struct((CELLS, 384), bf16), struct((CELLS, C), bf16)],
        [
            flags,
            sums,
            *others,
            x,
            above,
            below,
            group_gain.reshape(1, C),
            conv_weight.reshape(3, 3 * C, C),
            norm_gain.reshape(1, C),
            pad_query(spatial_query),
            spatial_kv,
        ],
        scratch=[pltpu.VMEM(((STRIP + 2) * W, 3 * C), bf16)],
        flops=2 * CELLS * C * C * 11,
        smem=1,
    )
    kv_far = swap(kv, 2)
    kv_near = swap(kv, 1)
    kv_far_near = swap(kv_far, 1)

    def attention(kv_parts, start):
        keys = sum(p.shape[0] for p in kv_parts)
        return call(
            functools.partial(attention_kernel, len(kv_parts), start is not None, CELLS),
            struct((CELLS, ACC_WIDTH), f32),
            [query, *kv_parts] + ([] if start is None else [start]),
            flops=2 * CELLS * keys * 512 * HEADS,
        )

    acc = attention([kv, kv_near], None)
    acc = attention([ref_kv, ref_near, ref_far, ref_far_near], acc)
    last = [kv_far, kv_far_near]
    mixed, sent = call(
        functools.partial(last_attention_kernel, len(last), CELLS),
        [struct((CELLS, C), bf16), struct((FRAMES * SENT, LANES), bf16)],
        [query, acc, hidden, pad_out(spatial_out), frame_gain.reshape(1, C), *last],
        scratch=[pltpu.VMEM((FRAMES * SENT, LANES), f32)],
        flops=2 * CELLS * 2 * CELLS * 512 * HEADS,
    )
    got = lax.all_to_all(
        sent.reshape(FRAMES, SENT, LANES), "frame", split_axis=0, concat_axis=0, tiled=True
    )
    back = call(
        temporal_kernel,
        struct((FRAMES * BACK, LANES), bf16),
        [got.reshape(FRAMES * SENT, LANES), pad_query(temporal_query), temporal_kv],
        scratch=[
            pltpu.VMEM((FRAMES * SENT, LANES), f32),
            pltpu.VMEM((CELLS, C), bf16),
            pltpu.VMEM((CELLS, 384), f32),
        ],
        flops=2 * CELLS * C * 960,
    )
    returned = lax.all_to_all(
        back.reshape(FRAMES, BACK, LANES), "frame", split_axis=0, concat_axis=0, tiled=True
    )
    output = call(
        final_kernel,
        struct((CELLS, C), bf16),
        [returned.reshape(FRAMES * BACK, LANES), pad_out(temporal_out), mixed],
        scratch=[
            pltpu.VMEM((FRAMES * BACK, LANES), f32),
            pltpu.VMEM((CELLS, 384), bf16),
        ],
        flops=2 * CELLS * C * 384,
    )
    return output.reshape(latent.shape)


def solution(mesh):
    return jax.shard_map(
        on_device,
        mesh=mesh,
        in_specs=(P("frame", "space", None, None), P("space", None, None)) + (P(),) * 12,
        out_specs=P("frame", "space", None, None),
        check_vma=False,
    )
```

```python
import functools

import jax
import jax.numpy as jnp
from jax import lax
from jax.experimental import pallas as pl
from jax.experimental.pallas import tpu as pltpu
from jax.sharding import PartitionSpec as P

HEADS = 4
HEAD_DIM = 80
GROUPS = 32
INNER = 320
C = 640
W = 48
STRIP = 12
CELLS = STRIP * W
FRAMES = 64
PLACES = CELLS // FRAMES
LANES = 128
SENT = 48
TILE = 768
HEAD = 512
CHUNKS = 4
BACK = 24

epsilon = 1e-05
QUERY_SCALE = HEAD_DIM**-0.5 * 1.4426950408889634

KEY_WINDOW = ((0, 128), (0, 256), (128, 256), (128, 384))
VALUE_WINDOW = ((256, 512), (384, 512), (384, 640), (512, 640))
ACC_AT = (0, 256, 384, 640)
ACC_WIDTH = 768

f32 = jnp.float32
bf16 = jnp.bfloat16


def lane_iota(width, start=0):
    return lax.broadcasted_iota(jnp.int32, (1, width), 1) + start


def layer_norm(values, factor):
    centre = jnp.mean(values, axis=-1, keepdims=True)
    shifted = values - centre
    spread = jnp.mean(shifted * shifted, axis=-1, keepdims=True)
    normed = shifted * lax.rsqrt(spread + epsilon)
    return normed if factor is None else normed * factor


def dot(a, b):
    return jnp.dot(a, b, preferred_element_type=f32)


def dot_t(a, b):
    return lax.dot_general(a, b, (((1,), (1,)), ((), ())), preferred_element_type=f32)


def vmem(count):
    return [pl.BlockSpec(memory_space=pltpu.VMEM)] * count


def call(body, outs, operands, scratch=(), smem=0, limit=8, anywhere=(), flops=0):
    single = not isinstance(outs, (list, tuple))
    specs = [pl.BlockSpec(memory_space=pltpu.SMEM)] * smem + vmem(len(operands) - smem)
    for i in anywhere:
        specs[i] = pl.BlockSpec(memory_space=pltpu.HBM)
    return pl.pallas_call(
        body,
        out_shape=outs,
        in_specs=specs,
        out_specs=vmem(1)[0] if single else vmem(len(outs)),
        scratch_shapes=list(scratch),
        compiler_params=pltpu.CompilerParams(vmem_limit_bytes=limit * 1024 * 1024),
        cost_estimate=pl.CostEstimate(flops=flops, bytes_accessed=0, transcendentals=0),
    )(*operands)


def pieces_of(value):
    high = value.astype(bf16).astype(f32)
    middle = (value - high).astype(bf16).astype(f32)
    return [high, middle, value - high - middle]


def stacked(rows, height):
    at = lax.broadcasted_iota(jnp.int32, (height, C), 0)
    result = jnp.zeros((height, C), f32)
    for i, row in enumerate(rows):
        result = jnp.where(at == i, row, result)
    return result


def sums_of(pieces):
    return pieces[0:1] + pieces[1:2] + pieces[2:3], pieces[3:4] + pieces[4:5] + pieces[5:6]


def stats_kernel(flags_ref, x_ref, sums_ref, near_ref, far_ref):
    total = jnp.zeros((1, C), f32)
    square = jnp.zeros((1, C), f32)
    for r in range(STRIP):
        v = x_ref[r * W : (r + 1) * W, :].astype(f32)
        total = total + jnp.sum(v, axis=0, keepdims=True)
        square = square + jnp.sum(v * v, axis=0, keepdims=True)
    per = C // GROUPS
    column_group = jnp.floor((lane_iota(C).astype(f32) + 0.5) * (1.0 / per))
    row_at = lax.broadcasted_iota(jnp.int32, (C, 1), 0).astype(f32)
    row_group = jnp.floor((row_at + 0.5) * (1.0 / per))
    same = jnp.where(row_group == column_group, 1.0, 0.0).astype(bf16)
    grouped = dot(stacked(pieces_of(total) + pieces_of(square), 16).astype(bf16), same)
    group_sum, group_sq = sums_of(grouped)
    sums_ref[...] = stacked([group_sum, group_sq], 8)
    near_ref[W:, :] = stacked(pieces_of(group_sum) + pieces_of(group_sq), 16).astype(bf16)
    odd = flags_ref[0, 2] > 0.5
    top = x_ref[0:W, :]
    bottom = x_ref[CELLS - W :, :]
    near_ref[0:W, :] = jnp.where(odd, top, bottom)
    far_ref[...] = jnp.where(odd, bottom, top)


def chip_sums_kernel(sums_ref, near_ref, edge_ref, sums_out, far_ref):
    group_sum, group_sq = sums_of(near_ref[W:, :].astype(f32))
    group_sum = group_sum + sums_ref[0:1]
    group_sq = group_sq + sums_ref[1:2]
    sums_out[...] = stacked([group_sum, group_sq], 8)
    far_ref[0:W, :] = edge_ref[...]
    far_ref[W:, :] = stacked(pieces_of(group_sum) + pieces_of(group_sq), 16).astype(bf16)


def reference_kv(weight, states):
    normed = layer_norm(states.astype(f32), None).astype(bf16)
    return dot_t(normed, weight[...]).astype(bf16)


def own_reference_kernel(
    flags_ref, states_ref, before_ref, key_ref, value_ref, out_ref, half_ref, weight
):
    half = CELLS // 2
    half_ref[...] = jnp.where(flags_ref[0, 3] > 0.5, states_ref[half:, :], states_ref[0:half, :])
    weight[0:INNER, :] = key_ref[...]
    weight[INNER:, :] = value_ref[...]
    out_ref[...] = reference_kv(weight, states_ref[...])


def far_reference_kernel(first_ref, second_ref, key_ref, value_ref, out_ref, *refs):
    chunk_refs, weight = refs[:CHUNKS], refs[CHUNKS]
    weight[0:INNER, :] = key_ref[...]
    weight[INNER:, :] = value_ref[...]
    half, size = CELLS // 2, CELLS // CHUNKS
    for i, ref in enumerate((first_ref, second_ref)):
        out = reference_kv(weight, ref[...])
        out_ref[i * half : (i + 1) * half, :] = out
        for j in range(half // size):
            chunk_refs[i * (half // size) + j][...] = out[j * size : (j + 1) * size]


def conv_kernel(
    flags_ref,
    sums_ref,
    x_ref,
    near_ref,
    far_ref,
    gain_ref,
    kernel_ref,
    norm_gain_ref,
    query_ref,
    key_ref,
    value_ref,
    hidden_out,
    query_out,
    kv_out,
    lhs,
    weight,
    taps,
    arrived,
):
    copies = [pltpu.make_async_copy(kernel_ref.at[a], taps.at[a], arrived.at[a]) for a in range(3)]
    for copy in copies:
        copy.start()
    weight[0:INNER, :] = key_ref[...]
    weight[INNER:, :] = value_ref[...]
    group_sum, group_sq = sums_of(far_ref[W:, :].astype(f32))
    members = float(4 * CELLS * (C // GROUPS))
    average = (group_sum + sums_ref[0:1]) / members
    variance = (group_sq + sums_ref[1:2]) / members - average * average
    factor = lax.rsqrt(variance + epsilon) * gain_ref[...]
    at = lax.broadcasted_iota(jnp.int32, (W, 1), 0)
    odd = flags_ref[0, 2] > 0.5

    def place(r, block, keep):
        v = (block.astype(f32) - average) * factor
        act = (0.5 * v) * (1.0 + jnp.tanh(0.5 * v))
        if keep is not None:
            act = jnp.where(keep > 0.5, act, 0.0)
        rows = slice(r * W, (r + 1) * W)
        lhs[rows, C : 2 * C] = act.astype(bf16)
        lhs[rows, 0:C] = jnp.where(at == 0, 0.0, pltpu.roll(act, 1, 0)).astype(bf16)
        lhs[rows, 2 * C :] = jnp.where(at == W - 1, 0.0, pltpu.roll(act, W - 1, 0)).astype(bf16)

    near, far = near_ref[0:W, :], far_ref[0:W, :]
    place(0, jnp.where(odd, near, far), flags_ref[0, 0])
    place(STRIP + 1, jnp.where(odd, far, near), flags_ref[0, 1])
    for r in range(STRIP):
        place(r + 1, x_ref[r * W : (r + 1) * W, :], None)
    for first in (0, CELLS // 2):
        rows = slice(first, first + CELLS // 2)
        total = None
        for a in range(3):
            if first == 0:
                copies[a].wait()
            part = dot(lhs[first + a * W : first + a * W + CELLS // 2, :], taps[a])
            total = part if total is None else total + part
        hidden_out[rows, :] = (x_ref[rows, :].astype(f32) + total).astype(bf16)
    normed = layer_norm(hidden_out[...].astype(f32), norm_gain_ref[...]).astype(bf16)
    kv_out[...] = dot_t(normed, weight[...]).astype(bf16)
    query_out[:, 0:INNER] = (dot_t(normed, query_ref[...]) * QUERY_SCALE).astype(bf16)
    query_out[:, INNER:] = jnp.zeros((CELLS, 64), bf16)


def head_query(query, h):
    low, high = KEY_WINDOW[h]
    lane = lane_iota(high - low, low)
    inside = (lane >= h * HEAD_DIM) & (lane < (h + 1) * HEAD_DIM)
    return jnp.where(inside, query[:, low:high], jnp.zeros((), bf16))


def inside_value(h):
    low, high = VALUE_WINDOW[h]
    lane = lane_iota(high - low, low)
    return (lane >= INNER + h * HEAD_DIM) & (lane < INNER + (h + 1) * HEAD_DIM)


def joined(kv_refs, ranges, scratch):
    at = 0
    for ref, (low, high) in zip(kv_refs, ranges):
        scratch[at : at + high - low, :] = ref[low:high, :]
        at += high - low
    return scratch


def attend(query, kv_ref, start):
    gathered = []
    keys = kv_ref.shape[0]
    for h in range(HEADS):
        key_low, key_high = KEY_WINDOW[h]
        low, high = VALUE_WINDOW[h]
        mine = head_query(query, h)
        inside = inside_value(h)
        acc = None if start is None else start(h)
        for first in range(0, keys, TILE):
            rows = slice(first, min(first + TILE, keys))
            weights = jnp.exp2(dot_t(mine, kv_ref[rows, key_low:key_high])).astype(bf16)
            values = jnp.where(inside, kv_ref[rows, low:high], jnp.ones((), bf16))
            part = dot(weights, values)
            acc = part if acc is None else acc + part
        gathered.append(acc)
    return gathered


def normalised(gathered):
    blocks = [None, None, None]
    for h in range(HEADS):
        low, high = VALUE_WINDOW[h]
        acc = gathered[h]
        spare = 0 if INNER + h * HEAD_DIM > low else high - low - 1
        result = acc * (1.0 / acc[:, spare : spare + 1])
        result = jnp.where(inside_value(h), result, 0.0)
        for b in range((high - low) // LANES):
            at = low // LANES + b - 2
            piece = result[:, b * LANES : (b + 1) * LANES]
            blocks[at] = piece if blocks[at] is None else blocks[at] + piece
    return blocks


def starting(acc_ref):
    return lambda h: acc_ref[:, ACC_AT[h] : ACC_AT[h] + VALUE_WINDOW[h][1] - VALUE_WINDOW[h][0]]


def attention_kernel(ranges, has_start, *refs):
    n_kv = len(ranges)
    query_ref = refs[0]
    start = starting(refs[1 + n_kv]) if has_start else None
    out_ref, scratch = refs[-2:]
    kv_ref = joined(refs[1 : 1 + n_kv], ranges, scratch)
    for h, acc in enumerate(attend(query_ref[...], kv_ref, start)):
        out_ref[:, ACC_AT[h] : ACC_AT[h] + acc.shape[1]] = acc


def last_attention_kernel(
    ranges,
    query_ref,
    acc_ref,
    first_ref,
    second_ref,
    hidden_ref,
    weight_ref,
    gain_ref,
    mixed_out,
    sent_out,
    rows,
    weight,
    scratch,
):
    kv_ref = joined((first_ref, second_ref), ranges, scratch)
    weight[0:64, :] = jnp.zeros((64, C), bf16)
    weight[64:, :] = weight_ref[...]
    blocks = normalised(attend(query_ref[...], kv_ref, starting(acc_ref)))
    update = None
    for b in range(3):
        part = dot(blocks[b].astype(bf16), weight[b * LANES : (b + 1) * LANES, :])
        update = part if update is None else update + part
    mixed = (hidden_ref[...].astype(f32) + update).astype(bf16)
    mixed_out[...] = mixed
    framed = layer_norm(mixed.astype(f32), gain_ref[...])
    for j in range(PLACES):
        for c in range(C // LANES):
            rows[pl.ds(j * 5 + c, FRAMES, stride=SENT + 1), :] = framed[
                j * FRAMES : (j + 1) * FRAMES, c * LANES : (c + 1) * LANES
            ]
    for r in range(PLACES * 5, SENT):
        rows[pl.ds(r, FRAMES, stride=SENT + 1), :] = jnp.zeros((FRAMES, LANES), f32)
    for g in range(FRAMES):
        sent_out[g * SENT : (g + 1) * SENT, :] = rows[
            g * (SENT + 1) : g * (SENT + 1) + SENT, :
        ].astype(bf16)


def temporal_kernel(
    got_ref, query_ref, key_ref, value_ref, out_ref, rows, tokens, result, weight
):
    weight[0:INNER, :] = key_ref[...]
    weight[INNER:, :] = value_ref[...]
    for g in range(FRAMES):
        rows[g * (SENT + 1) : g * (SENT + 1) + SENT, :] = got_ref[
            g * SENT : (g + 1) * SENT, :
        ].astype(f32)
    for j in range(PLACES):
        for c in range(C // LANES):
            tokens[j * FRAMES : (j + 1) * FRAMES, c * LANES : (c + 1) * LANES] = rows[
                pl.ds(j * 5 + c, FRAMES, stride=SENT + 1), :
            ].astype(bf16)
    query = (dot_t(tokens[...], query_ref[...]) * QUERY_SCALE).astype(bf16)
    query = jnp.concatenate([query, jnp.zeros((CELLS, 64), bf16)], axis=1)
    kv = dot_t(tokens[...], weight[...]).astype(bf16)
    span = 3 * FRAMES
    row_place = lax.broadcasted_iota(jnp.int32, (span, span), 0) // FRAMES
    column_place = lax.broadcasted_iota(jnp.int32, (span, span), 1) // FRAMES
    same = row_place == column_place
    for first in range(0, CELLS, span):
        gathered = []
        for h in range(HEADS):
            key_low, key_high = KEY_WINDOW[h]
            low, high = VALUE_WINDOW[h]
            scores = dot_t(
                head_query(query[first : first + span], h),
                kv[first : first + span, key_low:key_high],
            )
            weights = jnp.where(same, jnp.exp2(scores), 0.0).astype(bf16)
            values = jnp.where(
                inside_value(h), kv[first : first + span, low:high], jnp.ones((), bf16)
            )
            gathered.append(dot(weights, values))
        blocks = normalised(gathered)
        for b in range(3):
            result[first : first + span, b * LANES : (b + 1) * LANES] = blocks[b]
    for j in range(PLACES):
        cell = slice(j * FRAMES, (j + 1) * FRAMES)
        for b in range(2):
            rows[pl.ds(j * 2 + b, FRAMES, stride=BACK + 1), :] = result[
                cell, (1 + b) * LANES : (2 + b) * LANES
            ]
    for pair in range((PLACES + 1) // 2):
        half = result[2 * pair * FRAMES : (2 * pair + 1) * FRAMES, 0:LANES]
        if 2 * pair + 1 < PLACES:
            other = result[(2 * pair + 1) * FRAMES : (2 * pair + 2) * FRAMES, 0:LANES]
            half = half + pltpu.roll(other, LANES // 2, 1)
        rows[pl.ds(2 * PLACES + pair, FRAMES, stride=BACK + 1), :] = half
    rows[pl.ds(BACK - 1, FRAMES, stride=BACK + 1), :] = jnp.zeros((FRAMES, LANES), f32)
    for g in range(FRAMES):
        out_ref[g * BACK : (g + 1) * BACK, :] = rows[
            g * (BACK + 1) : g * (BACK + 1) + BACK, :
        ].astype(bf16)


def final_kernel(got_ref, weight_ref, mixed_ref, out_ref, rows, attended, weight):
    weight[0:64, :] = jnp.zeros((64, C), bf16)
    weight[64:, :] = weight_ref[...]
    for g in range(FRAMES):
        rows[g * (BACK + 1) : g * (BACK + 1) + BACK, :] = got_ref[
            g * BACK : (g + 1) * BACK, :
        ].astype(f32)
    upper = lane_iota(LANES) >= LANES // 2
    for j in range(PLACES):
        cell = slice(j * FRAMES, (j + 1) * FRAMES)
        for b in range(2):
            attended[cell, (1 + b) * LANES : (2 + b) * LANES] = rows[
                pl.ds(j * 2 + b, FRAMES, stride=BACK + 1), :
            ].astype(bf16)
        half = rows[pl.ds(2 * PLACES + j // 2, FRAMES, stride=BACK + 1), :]
        if j % 2:
            half = pltpu.roll(half, LANES // 2, 1)
        attended[cell, 0:LANES] = jnp.where(upper, half, 0.0).astype(bf16)
    update = dot(attended[...], weight[...])
    out_ref[...] = (mixed_ref[...].astype(f32) + update).astype(bf16)


def order_kernel(value_ref, before_ref, out_ref):
    pass


def after(value, before):
    return pl.pallas_call(
        order_kernel,
        out_shape=struct(value.shape, value.dtype),
        in_specs=[pl.BlockSpec(memory_space=pl.ANY)] * 2,
        out_specs=pl.BlockSpec(memory_space=pl.ANY),
        input_output_aliases={0: 0},
        compiler_params=pltpu.CompilerParams(vmem_limit_bytes=1 << 20),
        cost_estimate=pl.CostEstimate(flops=0, bytes_accessed=0, transcendentals=0),
    )(value, before)


def struct(shape, dtype):
    return jax.ShapeDtypeStruct(shape, dtype)


def on_device(
    latent,
    reference_states,
    group_gain,
    conv_weight,
    norm_gain,
    spatial_query,
    spatial_key,
    spatial_value,
    spatial_out,
    frame_gain,
    temporal_query,
    temporal_key,
    temporal_value,
    temporal_out,
):
    x = latent.reshape(CELLS, C)
    strip_at = lax.axis_index("space")
    odd_row = lax.axis_index("frame") // 8 % 2 == 1
    flags = (
        jnp.stack([strip_at > 0, strip_at < 3, strip_at % 2 == 1, odd_row])
        .astype(f32)
        .reshape(1, 4)
    )

    def swap(value, k):
        return lax.ppermute(value, "space", [(i, i ^ k) for i in range(4)])

    states = reference_states.reshape(CELLS, C)
    sums, near, edge = call(
        stats_kernel,
        [struct((8, C), f32), struct((W + 16, C), bf16), struct((W, C), bf16)],
        [flags, x],
        smem=1,
    )
    near = swap(near, 1)
    sums, far = call(
        chip_sums_kernel,
        [struct((8, C), f32), struct((W + 16, C), bf16)],
        [sums, near, edge],
    )
    far = swap(far, 3)

    ref_kv, half = call(
        own_reference_kernel,
        [struct((CELLS, C), bf16), struct((CELLS // 2, C), bf16)],
        [flags, states, sums, spatial_key.T, spatial_value.T],
        scratch=[pltpu.VMEM((C, C), bf16)],
        smem=1,
        flops=2*10**9,
    )
    half = swap(half, 2)

    hidden, query, kv = call(
        conv_kernel,
        [
            struct((CELLS, C), bf16),
            struct((CELLS, 384), bf16),
            struct((CELLS, C), bf16),
        ],
        [
            flags,
            sums,
            x,
            near,
            far,
            group_gain.reshape(1, C),
            conv_weight.reshape(3, 3 * C, C),
            norm_gain.reshape(1, C),
            spatial_query.T,
            spatial_key.T,
            spatial_value.T,
        ],
        scratch=[
            pltpu.VMEM(((STRIP + 2) * W, 3 * C), bf16),
            pltpu.VMEM((C, C), bf16),
            pltpu.VMEM((3, 3 * C, C), bf16),
            pltpu.SemaphoreType.DMA((3,)),
        ],
        smem=1,
        limit=46,
        anywhere=(6,),
    )
    ref_kv = after(ref_kv, query)
    ref_near = swap(ref_kv, 1)
    half = after(half, query)
    other_half = lax.ppermute(half, "frame", [(f, f ^ 8) for f in range(FRAMES)])
    kv_far = swap(kv, 2)
    kv_near = swap(kv, 1)

    def attention(kv_parts, start):
        ranges = [(low, high) for _, low, high in kv_parts]
        keys = sum(high - low for low, high in ranges)
        return call(
            functools.partial(attention_kernel, ranges, start is not None),
            struct((CELLS, ACC_WIDTH), f32),
            [query, *(part for part, _, _ in kv_parts)] + ([] if start is None else [start]),
            scratch=[pltpu.VMEM((keys, C), bf16)],
            limit=16,
        )

    acc = attention([(part, 0, CELLS) for part in (kv, kv_near, ref_kv, ref_near)], None)
    ref_far, *chunks = call(
        far_reference_kernel,
        [struct((CELLS, C), bf16)] + [struct((CELLS // CHUNKS, C), bf16)] * CHUNKS,
        [half, after(other_half, acc), spatial_key.T, spatial_value.T],
        scratch=[pltpu.VMEM((C, C), bf16)],
    )
    chunks = [swap(chunk, 1) for chunk in chunks]
    acc = attention([(ref_far, 0, HEAD)], acc)
    acc = attention(
        [(ref_far, HEAD, CELLS)] + [(chunk, 0, CELLS // CHUNKS) for chunk in chunks], acc
    )
    kv_far = after(kv_far, acc)
    kv_far_near = swap(kv_far, 1)
    acc = attention([(kv_far, 0, HEAD)], acc)
    ranges = [(HEAD, CELLS), (0, CELLS)]
    mixed, sent = call(
        functools.partial(last_attention_kernel, ranges),
        [struct((CELLS, C), bf16), struct((FRAMES * SENT, LANES), bf16)],
        [query, acc, kv_far, kv_far_near, hidden, spatial_out, frame_gain.reshape(1, C)],
        scratch=[
            pltpu.VMEM((FRAMES * (SENT + 1), LANES), f32),
            pltpu.VMEM((384, C), bf16),
            pltpu.VMEM((2 * CELLS - HEAD, C), bf16),
        ],
        limit=16,
    )
    got = lax.all_to_all(
        sent.reshape(FRAMES, SENT, LANES), "frame", split_axis=0, concat_axis=0, tiled=True
    )
    back = call(
        temporal_kernel,
        struct((FRAMES * BACK, LANES), bf16),
        [
            got.reshape(FRAMES * SENT, LANES),
            temporal_query.T,
            temporal_key.T,
            temporal_value.T,
        ],
        scratch=[
            pltpu.VMEM((FRAMES * (SENT + 1), LANES), f32),
            pltpu.VMEM((CELLS, C), bf16),
            pltpu.VMEM((CELLS, 384), f32),
            pltpu.VMEM((C, C), bf16),
        ],
    )
    returned = lax.all_to_all(
        back.reshape(FRAMES, BACK, LANES), "frame", split_axis=0, concat_axis=0, tiled=True
    )
    output = call(
        final_kernel,
        struct((CELLS, C), bf16),
        [returned.reshape(FRAMES * BACK, LANES), temporal_out, mixed],
        scratch=[
            pltpu.VMEM((FRAMES * (BACK + 1), LANES), f32),
            pltpu.VMEM((CELLS, 384), bf16),
            pltpu.VMEM((384, C), bf16),
        ],
    )
    return output.reshape(latent.shape)


def solution(mesh):
    return jax.shard_map(
        on_device,
        mesh=mesh,
        in_specs=(P("frame", "space", None, None), P("space", None, None)) + (P(),) * 12,
        out_specs=P("frame", "space", None, None),
        check_vma=False,
    )
```

```python
import functools

import jax
import jax.numpy as jnp
from jax import lax
from jax.experimental import pallas as pl
from jax.experimental.pallas import tpu as pltpu
from jax.sharding import PartitionSpec as P

HEADS = 4
HEAD_DIM = 80
GROUPS = 32
INNER = 320
C = 640
W = 48
STRIP = 12
CELLS = STRIP * W
FRAMES = 64
PLACES = CELLS // FRAMES
LANES = 128
SENT = 48
TILE = 768
HEAD = 512
FIRST = 256
PART = CELLS // 2
CHUNK = CELLS // 4
TAIL = 256
BACK = 24

epsilon = 1e-05
QUERY_SCALE = HEAD_DIM**-0.5 * 1.4426950408889634

KEY_WINDOW = ((0, 128), (0, 256), (128, 256), (128, 384))
VALUE_WINDOW = ((256, 512), (384, 512), (384, 640), (512, 640))
ACC_AT = (0, 256, 384, 640)
ACC_WIDTH = 768

f32 = jnp.float32
bf16 = jnp.bfloat16


def lane_iota(width, start=0):
    return lax.broadcasted_iota(jnp.int32, (1, width), 1) + start


def layer_norm(values, factor):
    centre = jnp.mean(values, axis=-1, keepdims=True)
    shifted = values - centre
    spread = jnp.mean(shifted * shifted, axis=-1, keepdims=True)
    normed = shifted * lax.rsqrt(spread + epsilon)
    return normed if factor is None else normed * factor


def dot(a, b):
    return jnp.dot(a, b, preferred_element_type=f32)


def dot_t(a, b):
    return lax.dot_general(a, b, (((1,), (1,)), ((), ())), preferred_element_type=f32)


def vmem(count):
    return [pl.BlockSpec(memory_space=pltpu.VMEM)] * count


def call(body, outs, operands, scratch=(), smem=0, limit=8, anywhere=(), flops=0):
    single = not isinstance(outs, (list, tuple))
    specs = [pl.BlockSpec(memory_space=pltpu.SMEM)] * smem + vmem(len(operands) - smem)
    for i in anywhere:
        specs[i] = pl.BlockSpec(memory_space=pltpu.HBM)
    return pl.pallas_call(
        body,
        out_shape=outs,
        in_specs=specs,
        out_specs=vmem(1)[0] if single else vmem(len(outs)),
        scratch_shapes=list(scratch),
        compiler_params=pltpu.CompilerParams(vmem_limit_bytes=limit * 1024 * 1024),
        cost_estimate=pl.CostEstimate(flops=flops, bytes_accessed=0, transcendentals=0),
    )(*operands)


def pieces_of(value):
    high = value.astype(bf16).astype(f32)
    middle = (value - high).astype(bf16).astype(f32)
    return [high, middle, value - high - middle]


def stacked(rows, height):
    at = lax.broadcasted_iota(jnp.int32, (height, C), 0)
    result = jnp.zeros((height, C), f32)
    for i, row in enumerate(rows):
        result = jnp.where(at == i, row, result)
    return result


def sums_of(pieces):
    return pieces[0:1] + pieces[1:2] + pieces[2:3], pieces[3:4] + pieces[4:5] + pieces[5:6]


def stats_kernel(flags_ref, x_ref, sums_ref, near_ref, far_ref):
    total = jnp.zeros((1, C), f32)
    square = jnp.zeros((1, C), f32)
    for r in range(STRIP):
        v = x_ref[r * W : (r + 1) * W, :].astype(f32)
        total = total + jnp.sum(v, axis=0, keepdims=True)
        square = square + jnp.sum(v * v, axis=0, keepdims=True)
    per = C // GROUPS
    column_group = jnp.floor((lane_iota(C).astype(f32) + 0.5) * (1.0 / per))
    row_at = lax.broadcasted_iota(jnp.int32, (C, 1), 0).astype(f32)
    row_group = jnp.floor((row_at + 0.5) * (1.0 / per))
    same = jnp.where(row_group == column_group, 1.0, 0.0).astype(bf16)
    grouped = dot(stacked(pieces_of(total) + pieces_of(square), 16).astype(bf16), same)
    group_sum, group_sq = sums_of(grouped)
    sums_ref[...] = stacked([group_sum, group_sq], 8)
    near_ref[W:, :] = stacked(pieces_of(group_sum) + pieces_of(group_sq), 16).astype(bf16)
    odd = flags_ref[0, 2] > 0.5
    top = x_ref[0:W, :]
    bottom = x_ref[CELLS - W :, :]
    near_ref[0:W, :] = jnp.where(odd, top, bottom)
    far_ref[...] = jnp.where(odd, bottom, top)


def chip_sums_kernel(sums_ref, near_ref, edge_ref, sums_out, far_ref):
    group_sum, group_sq = sums_of(near_ref[W:, :].astype(f32))
    group_sum = group_sum + sums_ref[0:1]
    group_sq = group_sq + sums_ref[1:2]
    sums_out[...] = stacked([group_sum, group_sq], 8)
    far_ref[0:W, :] = edge_ref[...]
    far_ref[W:, :] = stacked(pieces_of(group_sum) + pieces_of(group_sq), 16).astype(bf16)


def reference_kv(weight, states):
    normed = layer_norm(states.astype(f32), None).astype(bf16)
    return dot_t(normed, weight[...]).astype(bf16)


def own_reference_kernel(
    flags_ref, states_ref, before_ref, key_ref, value_ref, out_ref, half_ref, weight
):
    half = CELLS // 2
    half_ref[...] = jnp.where(flags_ref[0, 3] > 0.5, states_ref[half:, :], states_ref[0:half, :])
    weight[0:INNER, :] = key_ref[...]
    weight[INNER:, :] = value_ref[...]
    out_ref[...] = reference_kv(weight, states_ref[...])


def far_reference_kernel(first_ref, second_ref, key_ref, value_ref, out_ref, *refs):
    chunk_refs, weight = refs[:-1], refs[-1]
    weight[0:INNER, :] = key_ref[...]
    weight[INNER:, :] = value_ref[...]
    for i, ref in enumerate((first_ref, second_ref)):
        out_ref[i * PART : (i + 1) * PART, :] = reference_kv(weight, ref[...])
    for i, ref in enumerate(chunk_refs):
        ref[...] = out_ref[i * CHUNK : (i + 1) * CHUNK, :]


def parts_kernel(value_ref, out_ref, *part_refs):
    out_ref[...] = value_ref[...]
    size = FIRST // len(part_refs)
    for i, ref in enumerate(part_refs):
        ref[...] = value_ref[i * size : (i + 1) * size, :]


def conv_kernel(
    flags_ref,
    sums_ref,
    x_ref,
    near_ref,
    far_ref,
    gain_ref,
    kernel_ref,
    norm_gain_ref,
    query_ref,
    key_ref,
    value_ref,
    hidden_out,
    query_out,
    kv_out,
    first_out,
    second_out,
    lhs,
    weight,
):
    weight[0:INNER, :] = key_ref[...]
    weight[INNER:, :] = value_ref[...]
    group_sum, group_sq = sums_of(far_ref[W:, :].astype(f32))
    members = float(4 * CELLS * (C // GROUPS))
    average = (group_sum + sums_ref[0:1]) / members
    variance = (group_sq + sums_ref[1:2]) / members - average * average
    factor = lax.rsqrt(variance + epsilon) * gain_ref[...].reshape(1, C)
    at = lax.broadcasted_iota(jnp.int32, (W, 1), 0)
    odd = flags_ref[0, 2] > 0.5

    def place(r, block, keep):
        v = (block.astype(f32) - average) * factor
        act = (0.5 * v) * (1.0 + jnp.tanh(0.5 * v))
        if keep is not None:
            act = jnp.where(keep > 0.5, act, 0.0)
        rows = slice(r * W, (r + 1) * W)
        lhs[rows, C : 2 * C] = act.astype(bf16)
        lhs[rows, 0:C] = jnp.where(at == 0, 0.0, pltpu.roll(act, 1, 0)).astype(bf16)
        lhs[rows, 2 * C :] = jnp.where(at == W - 1, 0.0, pltpu.roll(act, W - 1, 0)).astype(bf16)

    near, far = near_ref[0:W, :], far_ref[0:W, :]
    place(0, jnp.where(odd, near, far), flags_ref[0, 0])
    place(STRIP + 1, jnp.where(odd, far, near), flags_ref[0, 1])
    for r in range(STRIP):
        place(r + 1, x_ref[r * W : (r + 1) * W, :], None)
    for first in (0, CELLS // 2):
        rows = slice(first, first + CELLS // 2)
        total = None
        for a in range(3):
            part = dot(lhs[first + a * W : first + a * W + CELLS // 2, :], kernel_ref[a])
            total = part if total is None else total + part
        hidden_out[rows, :] = (x_ref[rows, :].astype(f32) + total).astype(bf16)
    normed = layer_norm(hidden_out[...].astype(f32), norm_gain_ref[...].reshape(1, C)).astype(bf16)
    kv = dot_t(normed, weight[...]).astype(bf16)
    kv_out[...] = kv
    first_out[...] = kv[0:FIRST]
    second_out[...] = kv[FIRST:]
    query_out[:, 0:INNER] = (dot_t(normed, query_ref[...]) * QUERY_SCALE).astype(bf16)
    query_out[:, INNER:] = jnp.zeros((CELLS, 64), bf16)


def head_query(query, h):
    low, high = KEY_WINDOW[h]
    lane = lane_iota(high - low, low)
    inside = (lane >= h * HEAD_DIM) & (lane < (h + 1) * HEAD_DIM)
    return jnp.where(inside, query[:, low:high], jnp.zeros((), bf16))


def inside_value(h):
    low, high = VALUE_WINDOW[h]
    lane = lane_iota(high - low, low)
    return (lane >= INNER + h * HEAD_DIM) & (lane < INNER + (h + 1) * HEAD_DIM)


def joined(kv_refs, ranges, scratch):
    at = 0
    for ref, (low, high) in zip(kv_refs, ranges):
        scratch[at : at + high - low, :] = ref[low:high, :]
        at += high - low
    return scratch


def attend(query, kv_ref, start):
    gathered = []
    keys = kv_ref.shape[0]
    for h in range(HEADS):
        key_low, key_high = KEY_WINDOW[h]
        low, high = VALUE_WINDOW[h]
        mine = head_query(query, h)
        inside = inside_value(h)
        acc = None if start is None else start(h)
        for first in range(0, keys, TILE):
            rows = slice(first, min(first + TILE, keys))
            weights = jnp.exp2(dot_t(mine, kv_ref[rows, key_low:key_high])).astype(bf16)
            values = jnp.where(inside, kv_ref[rows, low:high], jnp.ones((), bf16))
            part = dot(weights, values)
            acc = part if acc is None else acc + part
        gathered.append(acc)
    return gathered


def normalised(gathered):
    blocks = [None, None, None]
    for h in range(HEADS):
        low, high = VALUE_WINDOW[h]
        acc = gathered[h]
        spare = 0 if INNER + h * HEAD_DIM > low else high - low - 1
        result = acc * (1.0 / acc[:, spare : spare + 1])
        result = jnp.where(inside_value(h), result, 0.0)
        for b in range((high - low) // LANES):
            at = low // LANES + b - 2
            piece = result[:, b * LANES : (b + 1) * LANES]
            blocks[at] = piece if blocks[at] is None else blocks[at] + piece
    return blocks


def starting(acc_ref):
    return lambda h: acc_ref[:, ACC_AT[h] : ACC_AT[h] + VALUE_WINDOW[h][1] - VALUE_WINDOW[h][0]]


def attention_kernel(ranges, has_start, *refs):
    n_kv = len(ranges)
    query_ref = refs[0]
    start = starting(refs[1 + n_kv]) if has_start else None
    out_ref, scratch = refs[-2:]
    kv_ref = joined(refs[1 : 1 + n_kv], ranges, scratch)
    for h, acc in enumerate(attend(query_ref[...], kv_ref, start)):
        out_ref[:, ACC_AT[h] : ACC_AT[h] + acc.shape[1]] = acc


def last_attention_kernel(
    ranges,
    query_ref,
    acc_ref,
    first_ref,
    second_ref,
    hidden_ref,
    weight_ref,
    gain_ref,
    mixed_out,
    sent_out,
    rows,
    weight,
    scratch,
):
    kv_ref = joined((first_ref, second_ref), ranges, scratch)
    weight[0:64, :] = jnp.zeros((64, C), bf16)
    weight[64:, :] = weight_ref[...]
    blocks = normalised(attend(query_ref[...], kv_ref, starting(acc_ref)))
    update = None
    for b in range(3):
        part = dot(blocks[b].astype(bf16), weight[b * LANES : (b + 1) * LANES, :])
        update = part if update is None else update + part
    mixed = (hidden_ref[...].astype(f32) + update).astype(bf16)
    mixed_out[...] = mixed
    framed = layer_norm(mixed.astype(f32), gain_ref[...].reshape(1, C))
    for j in range(PLACES):
        for c in range(C // LANES):
            rows[pl.ds(j * 5 + c, FRAMES, stride=SENT + 1), :] = framed[
                j * FRAMES : (j + 1) * FRAMES, c * LANES : (c + 1) * LANES
            ]
    for r in range(PLACES * 5, SENT):
        rows[pl.ds(r, FRAMES, stride=SENT + 1), :] = jnp.zeros((FRAMES, LANES), f32)
    for g in range(FRAMES):
        sent_out[g * SENT : (g + 1) * SENT, :] = rows[
            g * (SENT + 1) : g * (SENT + 1) + SENT, :
        ].astype(bf16)


def temporal_kernel(
    got_ref, query_ref, key_ref, value_ref, out_ref, rows, tokens, result, weight
):
    weight[0:INNER, :] = key_ref[...]
    weight[INNER:, :] = value_ref[...]
    for g in range(FRAMES):
        rows[g * (SENT + 1) : g * (SENT + 1) + SENT, :] = got_ref[
            g * SENT : (g + 1) * SENT, :
        ].astype(f32)
    for j in range(PLACES):
        for c in range(C // LANES):
            tokens[j * FRAMES : (j + 1) * FRAMES, c * LANES : (c + 1) * LANES] = rows[
                pl.ds(j * 5 + c, FRAMES, stride=SENT + 1), :
            ].astype(bf16)
    query = (dot_t(tokens[...], query_ref[...]) * QUERY_SCALE).astype(bf16)
    query = jnp.concatenate([query, jnp.zeros((CELLS, 64), bf16)], axis=1)
    kv = dot_t(tokens[...], weight[...]).astype(bf16)
    span = 3 * FRAMES
    row_place = lax.broadcasted_iota(jnp.int32, (span, span), 0) // FRAMES
    column_place = lax.broadcasted_iota(jnp.int32, (span, span), 1) // FRAMES
    same = row_place == column_place
    for first in range(0, CELLS, span):
        gathered = []
        for h in range(HEADS):
            key_low, key_high = KEY_WINDOW[h]
            low, high = VALUE_WINDOW[h]
            scores = dot_t(
                head_query(query[first : first + span], h),
                kv[first : first + span, key_low:key_high],
            )
            weights = jnp.where(same, jnp.exp2(scores), 0.0).astype(bf16)
            values = jnp.where(
                inside_value(h), kv[first : first + span, low:high], jnp.ones((), bf16)
            )
            gathered.append(dot(weights, values))
        blocks = normalised(gathered)
        for b in range(3):
            result[first : first + span, b * LANES : (b + 1) * LANES] = blocks[b]
    for j in range(PLACES):
        cell = slice(j * FRAMES, (j + 1) * FRAMES)
        for b in range(2):
            rows[pl.ds(j * 2 + b, FRAMES, stride=BACK + 1), :] = result[
                cell, (1 + b) * LANES : (2 + b) * LANES
            ]
    for pair in range((PLACES + 1) // 2):
        half = result[2 * pair * FRAMES : (2 * pair + 1) * FRAMES, 0:LANES]
        if 2 * pair + 1 < PLACES:
            other = result[(2 * pair + 1) * FRAMES : (2 * pair + 2) * FRAMES, 0:LANES]
            half = half + pltpu.roll(other, LANES // 2, 1)
        rows[pl.ds(2 * PLACES + pair, FRAMES, stride=BACK + 1), :] = half
    rows[pl.ds(BACK - 1, FRAMES, stride=BACK + 1), :] = jnp.zeros((FRAMES, LANES), f32)
    for g in range(FRAMES):
        out_ref[g * BACK : (g + 1) * BACK, :] = rows[
            g * (BACK + 1) : g * (BACK + 1) + BACK, :
        ].astype(bf16)


def final_kernel(got_ref, weight_ref, mixed_ref, out_ref, rows, attended, weight):
    weight[0:64, :] = jnp.zeros((64, C), bf16)
    weight[64:, :] = weight_ref[...]
    for g in range(FRAMES):
        rows[g * (BACK + 1) : g * (BACK + 1) + BACK, :] = got_ref[
            g * BACK : (g + 1) * BACK, :
        ].astype(f32)
    upper = lane_iota(LANES) >= LANES // 2
    for j in range(PLACES):
        cell = slice(j * FRAMES, (j + 1) * FRAMES)
        for b in range(2):
            attended[cell, (1 + b) * LANES : (2 + b) * LANES] = rows[
                pl.ds(j * 2 + b, FRAMES, stride=BACK + 1), :
            ].astype(bf16)
        half = rows[pl.ds(2 * PLACES + j // 2, FRAMES, stride=BACK + 1), :]
        if j % 2:
            half = pltpu.roll(half, LANES // 2, 1)
        attended[cell, 0:LANES] = jnp.where(upper, half, 0.0).astype(bf16)
    update = dot(attended[...], weight[...])
    out_ref[...] = (mixed_ref[...].astype(f32) + update).astype(bf16)


def order_kernel(value_ref, before_ref, out_ref):
    pass


def after(value, before):
    return pl.pallas_call(
        order_kernel,
        out_shape=struct(value.shape, value.dtype),
        in_specs=[pl.BlockSpec(memory_space=pl.ANY)] * 2,
        out_specs=pl.BlockSpec(memory_space=pl.ANY),
        input_output_aliases={0: 0},
        compiler_params=pltpu.CompilerParams(vmem_limit_bytes=1 << 20),
        cost_estimate=pl.CostEstimate(flops=0, bytes_accessed=0, transcendentals=0),
    )(value, before)


def struct(shape, dtype):
    return jax.ShapeDtypeStruct(shape, dtype)


def on_device(
    latent,
    reference_states,
    group_gain,
    conv_weight,
    norm_gain,
    spatial_query,
    spatial_key,
    spatial_value,
    spatial_out,
    frame_gain,
    temporal_query,
    temporal_key,
    temporal_value,
    temporal_out,
):
    x = latent.reshape(CELLS, C)
    strip_at = lax.axis_index("space")
    odd_row = lax.axis_index("frame") // 8 % 2 == 1
    flags = (
        jnp.stack([strip_at > 0, strip_at < 3, strip_at % 2 == 1, odd_row])
        .astype(f32)
        .reshape(1, 4)
    )

    def swap(value, k):
        return lax.ppermute(value, "space", [(i, i ^ k) for i in range(4)])

    states = reference_states.reshape(CELLS, C)
    sums, near, edge = call(
        stats_kernel,
        [struct((8, C), f32), struct((W + 16, C), bf16), struct((W, C), bf16)],
        [flags, x],
        smem=1,
        flops=2 * 10**9,
    )
    near = swap(near, 1)
    sums, far = call(
        chip_sums_kernel,
        [struct((8, C), f32), struct((W + 16, C), bf16)],
        [sums, near, edge],
        flops=2 * 10**9,
    )
    far = swap(far, 3)

    ref_kv, half = call(
        own_reference_kernel,
        [struct((CELLS, C), bf16), struct((CELLS // 2, C), bf16)],
        [flags, states, sums, spatial_key.T, spatial_value.T],
        scratch=[pltpu.VMEM((C, C), bf16)],
        smem=1,
        flops=2 * 10**9,
        limit=8,
    )
    half = swap(half, 2)

    hidden, query, kv, first, second = call(
        conv_kernel,
        [
            struct((CELLS, C), bf16),
            struct((CELLS, 384), bf16),
            struct((CELLS, C), bf16),
            struct((FIRST, C), bf16),
            struct((CELLS - FIRST, C), bf16),
        ],
        [
            flags,
            sums,
            x,
            near,
            far,
            group_gain,
            conv_weight.reshape(3, 3 * C, C),
            norm_gain,
            spatial_query.T,
            spatial_key.T,
            spatial_value.T,
        ],
        scratch=[
            pltpu.VMEM(((STRIP + 2) * W, 3 * C), bf16),
            pltpu.VMEM((C, C), bf16),
        ],
        smem=1,
        limit=16,
    )
    ref_kv = after(ref_kv, query)
    ref_near = swap(ref_kv, 1)
    half = after(half, query)
    other_half = lax.ppermute(half, "frame", [(f, f ^ 8) for f in range(FRAMES)])
    first = swap(first, 2)
    second = swap(second, 2)
    kv_near = swap(kv, 1)

    def attention(kv_parts, start):
        ranges = [(low, high) for _, low, high in kv_parts]
        keys = sum(high - low for low, high in ranges)
        return call(
            functools.partial(attention_kernel, ranges, start is not None),
            struct((CELLS, ACC_WIDTH), f32),
            [query, *(part for part, _, _ in kv_parts)] + ([] if start is None else [start]),
            scratch=[pltpu.VMEM((keys, C), bf16)],
            limit=16,
        )

    acc = attention([(part, 0, CELLS) for part in (kv, kv_near, ref_kv, ref_near)], None)
    chunk = struct((CHUNK, C), bf16)
    ref_far, *ref_far_near = call(
        far_reference_kernel,
        [struct((CELLS, C), bf16)] + [chunk] * (CELLS // CHUNK),
        [half, after(other_half, acc), spatial_key.T, spatial_value.T],
        scratch=[pltpu.VMEM((C, C), bf16)],
    )
    ref_far_near = [swap(part, 1) for part in ref_far_near]
    first, *first_near = call(
        parts_kernel,
        [struct((FIRST, C), bf16)] + [struct((FIRST // 2, C), bf16)] * 2,
        [after(first, ref_far)],
    )
    first_near = [swap(part, 1) for part in first_near]
    acc = attention([(ref_far, 0, HEAD)], acc)
    acc = attention(
        [(ref_far, HEAD, CELLS), (first, 0, FIRST)]
        + [(part, 0, part.shape[0]) for part in ref_far_near + first_near],
        acc,
    )
    second = after(second, acc)
    second_near = swap(second, 1)
    acc = attention([(second, 0, TAIL)], acc)
    ranges = [(TAIL, CELLS - FIRST), (0, CELLS - FIRST)]
    mixed, sent = call(
        functools.partial(last_attention_kernel, ranges),
        [struct((CELLS, C), bf16), struct((FRAMES * SENT, LANES), bf16)],
        [query, acc, second, second_near, hidden, spatial_out, frame_gain],
        scratch=[
            pltpu.VMEM((FRAMES * (SENT + 1), LANES), f32),
            pltpu.VMEM((384, C), bf16),
            pltpu.VMEM((2 * (CELLS - FIRST) - TAIL, C), bf16),
        ],
        limit=16,
    )
    got = lax.all_to_all(
        sent.reshape(FRAMES, SENT, LANES), "frame", split_axis=0, concat_axis=0, tiled=True
    )
    back = call(
        temporal_kernel,
        struct((FRAMES * BACK, LANES), bf16),
        [
            got.reshape(FRAMES * SENT, LANES),
            temporal_query.T,
            temporal_key.T,
            temporal_value.T,
        ],
        scratch=[
            pltpu.VMEM((FRAMES * (SENT + 1), LANES), f32),
            pltpu.VMEM((CELLS, C), bf16),
            pltpu.VMEM((CELLS, 384), f32),
            pltpu.VMEM((C, C), bf16),
        ],
    )
    returned = lax.all_to_all(
        back.reshape(FRAMES, BACK, LANES), "frame", split_axis=0, concat_axis=0, tiled=True
    )
    output = call(
        final_kernel,
        struct((CELLS, C), bf16),
        [returned.reshape(FRAMES * BACK, LANES), temporal_out, mixed],
        scratch=[
            pltpu.VMEM((FRAMES * (BACK + 1), LANES), f32),
            pltpu.VMEM((CELLS, 384), bf16),
            pltpu.VMEM((384, C), bf16),
        ],
    )
    return output.reshape(latent.shape)


def solution(mesh):
    return jax.shard_map(
        on_device,
        mesh=mesh,
        in_specs=(P("frame", "space", None, None), P("space", None, None)) + (P(),) * 12,
        out_specs=P("frame", "space", None, None),
        check_vma=False,
    )
```

```python
import functools

import jax
import jax.numpy as jnp
from jax import lax
from jax.experimental import pallas as pl
from jax.experimental.pallas import tpu as pltpu
from jax.sharding import PartitionSpec as P

HEADS = 4
HEAD_DIM = 80
GROUPS = 32
INNER = 320
C = 640
W = 48
STRIP = 12
CELLS = STRIP * W
FRAMES = 64
PLACES = CELLS // FRAMES
LANES = 128
SENT = 48
TILE = 768
EARLY = 224
HEAD = 48
FIRST = 320
PART = CELLS // 2
BACK = 24

epsilon = 1e-05
QUERY_SCALE = HEAD_DIM**-0.5 * 1.4426950408889634

KEY_WINDOW = ((0, 128), (0, 256), (128, 256), (128, 384))
VALUE_WINDOW = ((256, 512), (384, 512), (384, 640), (512, 640))
ACC_AT = (0, 256, 384, 640)
ACC_WIDTH = 768

f32 = jnp.float32
bf16 = jnp.bfloat16


def lane_iota(width, start=0):
    return lax.broadcasted_iota(jnp.int32, (1, width), 1) + start


def layer_norm(values, factor):
    centre = jnp.mean(values, axis=-1, keepdims=True)
    shifted = values - centre
    spread = jnp.mean(shifted * shifted, axis=-1, keepdims=True)
    normed = shifted * lax.rsqrt(spread + epsilon)
    return normed if factor is None else normed * factor


def dot(a, b):
    return jnp.dot(a, b, preferred_element_type=f32)


def dot_t(a, b):
    return lax.dot_general(a, b, (((1,), (1,)), ((), ())), preferred_element_type=f32)


def vmem(count):
    return [pl.BlockSpec(memory_space=pltpu.VMEM)] * count


def call(body, outs, operands, scratch=(), smem=0, limit=8, anywhere=(), flops=0):
    single = not isinstance(outs, (list, tuple))
    specs = [pl.BlockSpec(memory_space=pltpu.SMEM)] * smem + vmem(len(operands) - smem)
    for i in anywhere:
        specs[i] = pl.BlockSpec(memory_space=pl.ANY)
    return pl.pallas_call(
        body,
        out_shape=outs,
        in_specs=specs,
        out_specs=vmem(1)[0] if single else vmem(len(outs)),
        scratch_shapes=list(scratch),
        compiler_params=pltpu.CompilerParams(vmem_limit_bytes=limit * 1024 * 1024),
        cost_estimate=pl.CostEstimate(flops=flops, bytes_accessed=0, transcendentals=0),
    )(*operands)


def pieces_of(value):
    high = value.astype(bf16).astype(f32)
    middle = (value - high).astype(bf16).astype(f32)
    return [high, middle, value - high - middle]


def stacked(rows, height):
    at = lax.broadcasted_iota(jnp.int32, (height, C), 0)
    result = jnp.zeros((height, C), f32)
    for i, row in enumerate(rows):
        result = jnp.where(at == i, row, result)
    return result


def sums_of(pieces):
    return pieces[0:1] + pieces[1:2] + pieces[2:3], pieces[3:4] + pieces[4:5] + pieces[5:6]


def stats_kernel(flags_ref, x_ref, sums_ref, near_ref, far_ref):
    total = jnp.zeros((1, C), f32)
    square = jnp.zeros((1, C), f32)
    for r in range(STRIP):
        v = x_ref[r * W : (r + 1) * W, :].astype(f32)
        total = total + jnp.sum(v, axis=0, keepdims=True)
        square = square + jnp.sum(v * v, axis=0, keepdims=True)
    per = C // GROUPS
    column_group = jnp.floor((lane_iota(C).astype(f32) + 0.5) * (1.0 / per))
    row_at = lax.broadcasted_iota(jnp.int32, (C, 1), 0).astype(f32)
    row_group = jnp.floor((row_at + 0.5) * (1.0 / per))
    same = jnp.where(row_group == column_group, 1.0, 0.0).astype(bf16)
    grouped = dot(stacked(pieces_of(total) + pieces_of(square), 16).astype(bf16), same)
    group_sum, group_sq = sums_of(grouped)
    sums_ref[...] = stacked([group_sum, group_sq], 8)
    near_ref[W:, :] = stacked(pieces_of(group_sum) + pieces_of(group_sq), 16).astype(bf16)
    odd = flags_ref[0, 2] > 0.5
    top = x_ref[0:W, :]
    bottom = x_ref[CELLS - W :, :]
    near_ref[0:W, :] = jnp.where(odd, top, bottom)
    far_ref[...] = jnp.where(odd, bottom, top)


def chip_sums_kernel(sums_ref, near_ref, edge_ref, sums_out, far_ref):
    group_sum, group_sq = sums_of(near_ref[W:, :].astype(f32))
    group_sum = group_sum + sums_ref[0:1]
    group_sq = group_sq + sums_ref[1:2]
    sums_out[...] = stacked([group_sum, group_sq], 8)
    far_ref[0:W, :] = edge_ref[...]
    far_ref[W:, :] = stacked(pieces_of(group_sum) + pieces_of(group_sq), 16).astype(bf16)


def reference_kv(weight, states):
    normed = layer_norm(states.astype(f32), None).astype(bf16)
    return dot_t(normed, weight[...]).astype(bf16)


def reference_kernel(
    flags_ref, states_ref, before_ref, key_ref, value_ref, out_ref, half_ref, weight
):
    weight[0:INNER, :] = key_ref[...]
    weight[INNER:, :] = value_ref[...]
    out_ref[...] = reference_kv(weight, states_ref[...])
    half_ref[...] = jnp.where(flags_ref[0, 3] > 0.5, out_ref[PART:, :], out_ref[0:PART, :])


def parts_kernel(first_ref, second_ref, before_ref, *part_refs):
    for i, part_ref in enumerate(part_refs):
        ref = (first_ref, second_ref)[i // 2]
        size = part_ref.shape[0]
        part_ref[...] = ref[i % 2 * size : (i % 2 + 1) * size, :]


def joined_weights(weight, key_ref, value_ref, query_ref):
    weight[0:INNER, :] = key_ref[...]
    weight[INNER:C, :] = value_ref[...]
    weight[C:, :] = query_ref[...]


def conv_kernel(
    flags_ref,
    sums_ref,
    x_ref,
    near_ref,
    far_ref,
    gain_ref,
    kernel_ref,
    norm_gain_ref,
    query_ref,
    key_ref,
    value_ref,
    hidden_out,
    query_out,
    kv_out,
    low_out,
    high_out,
    first_out,
    second_out,
    lhs,
    weight,
):
    joined_weights(weight, key_ref, value_ref, query_ref)
    group_sum, group_sq = sums_of(far_ref[W:, :].astype(f32))
    members = float(4 * CELLS * (C // GROUPS))
    average = (group_sum + sums_ref[0:1]) / members
    variance = (group_sq + sums_ref[1:2]) / members - average * average
    factor = lax.rsqrt(variance + epsilon) * gain_ref[...].reshape(1, C)
    at = lax.broadcasted_iota(jnp.int32, (W, 1), 0)
    odd = flags_ref[0, 2] > 0.5

    def place(r, block, keep):
        v = (block.astype(f32) - average) * factor
        act = (0.5 * v) * (1.0 + jnp.tanh(0.5 * v))
        if keep is not None:
            act = jnp.where(keep > 0.5, act, 0.0)
        rows = slice(r * W, (r + 1) * W)
        lhs[rows, C : 2 * C] = act.astype(bf16)
        lhs[rows, 0:C] = jnp.where(at == 0, 0.0, pltpu.roll(act, 1, 0)).astype(bf16)
        lhs[rows, 2 * C :] = jnp.where(at == W - 1, 0.0, pltpu.roll(act, W - 1, 0)).astype(bf16)

    near, far = near_ref[0:W, :], far_ref[0:W, :]
    place(0, jnp.where(odd, near, far), flags_ref[0, 0])
    place(STRIP + 1, jnp.where(odd, far, near), flags_ref[0, 1])
    for r in range(STRIP):
        place(r + 1, x_ref[r * W : (r + 1) * W, :], None)
    for first in (0, CELLS // 2):
        rows = slice(first, first + CELLS // 2)
        total = None
        for a in range(3):
            part = dot(lhs[first + a * W : first + a * W + CELLS // 2, :], kernel_ref[a])
            total = part if total is None else total + part
        hidden_out[rows, :] = (x_ref[rows, :].astype(f32) + total).astype(bf16)
    normed = layer_norm(hidden_out[...].astype(f32), norm_gain_ref[...].reshape(1, C)).astype(bf16)
    projected = dot_t(normed, weight[...])
    kv = projected[:, 0:C].astype(bf16)
    kv_out[...] = kv
    low_out[...] = kv[0:PART]
    high_out[...] = kv[PART:]
    first_out[...] = kv[0:FIRST]
    second_out[...] = kv[FIRST:]
    query_out[:, 0:INNER] = (projected[:, C:] * QUERY_SCALE).astype(bf16)
    query_out[:, INNER:] = jnp.zeros((CELLS, 64), bf16)


def head_query(query, h):
    low, high = KEY_WINDOW[h]
    lane = lane_iota(high - low, low)
    inside = (lane >= h * HEAD_DIM) & (lane < (h + 1) * HEAD_DIM)
    return jnp.where(inside, query[:, low:high], jnp.zeros((), bf16))


def inside_value(h):
    low, high = VALUE_WINDOW[h]
    lane = lane_iota(high - low, low)
    return (lane >= INNER + h * HEAD_DIM) & (lane < INNER + (h + 1) * HEAD_DIM)


def joined(kv_refs, ranges, scratch):
    at = 0
    for ref, (low, high) in zip(kv_refs, ranges):
        scratch[at : at + high - low, :] = ref[low:high, :]
        at += high - low
    return scratch


def attend(query, kv_ref, start):
    gathered = []
    keys = kv_ref.shape[0]
    for h in range(HEADS):
        key_low, key_high = KEY_WINDOW[h]
        low, high = VALUE_WINDOW[h]
        mine = head_query(query, h)
        inside = inside_value(h)
        acc = None if start is None else start(h)
        for first in range(0, keys, TILE):
            rows = slice(first, min(first + TILE, keys))
            weights = jnp.exp2(dot_t(mine, kv_ref[rows, key_low:key_high])).astype(bf16)
            values = jnp.where(inside, kv_ref[rows, low:high], jnp.ones((), bf16))
            part = dot(weights, values)
            acc = part if acc is None else acc + part
        gathered.append(acc)
    return gathered


def normalised(gathered):
    blocks = [None, None, None]
    for h in range(HEADS):
        low, high = VALUE_WINDOW[h]
        acc = gathered[h]
        spare = 0 if INNER + h * HEAD_DIM > low else high - low - 1
        result = acc * (1.0 / acc[:, spare : spare + 1])
        result = jnp.where(inside_value(h), result, 0.0)
        for b in range((high - low) // LANES):
            at = low // LANES + b - 2
            piece = result[:, b * LANES : (b + 1) * LANES]
            blocks[at] = piece if blocks[at] is None else blocks[at] + piece
    return blocks


def starting(acc_ref):
    return lambda h: acc_ref[:, ACC_AT[h] : ACC_AT[h] + VALUE_WINDOW[h][1] - VALUE_WINDOW[h][0]]


def attention_kernel(ranges, has_start, *refs):
    n_kv = len(ranges)
    query_ref = refs[0]
    start = starting(refs[1 + n_kv]) if has_start else None
    out_ref, scratch = refs[-2:]
    kv_ref = joined(refs[1 : 1 + n_kv], ranges, scratch)
    for h, acc in enumerate(attend(query_ref[...], kv_ref, start)):
        out_ref[:, ACC_AT[h] : ACC_AT[h] + acc.shape[1]] = acc


def last_attention_kernel(
    query_ref,
    acc_ref,
    kv_ref,
    hidden_ref,
    weight_ref,
    gain_ref,
    mixed_out,
    sent_out,
    rows,
    weight,
):
    weight[0:64, :] = jnp.zeros((64, C), bf16)
    weight[64:, :] = weight_ref[...]
    blocks = normalised(attend(query_ref[...], kv_ref, starting(acc_ref)))
    attended = jnp.concatenate([block.astype(bf16) for block in blocks], axis=1)
    update = dot(attended, weight[...])
    mixed = (hidden_ref[...].astype(f32) + update).astype(bf16)
    mixed_out[...] = mixed
    framed = layer_norm(mixed.astype(f32), gain_ref[...].reshape(1, C))
    for j in range(PLACES):
        for c in range(C // LANES):
            rows[pl.ds(j * 5 + c, FRAMES, stride=SENT + 1), :] = framed[
                j * FRAMES : (j + 1) * FRAMES, c * LANES : (c + 1) * LANES
            ]
    for r in range(PLACES * 5, SENT):
        rows[pl.ds(r, FRAMES, stride=SENT + 1), :] = jnp.zeros((FRAMES, LANES), f32)
    for g in range(FRAMES):
        sent_out[g * SENT : (g + 1) * SENT, :] = rows[
            g * (SENT + 1) : g * (SENT + 1) + SENT, :
        ].astype(bf16)


def temporal_kernel(
    got_ref, query_ref, key_ref, value_ref, out_ref, rows, tokens, result, weight
):
    joined_weights(weight, key_ref, value_ref, query_ref)
    for g in range(FRAMES):
        rows[g * (SENT + 1) : g * (SENT + 1) + SENT, :] = got_ref[
            g * SENT : (g + 1) * SENT, :
        ].astype(f32)
    for j in range(PLACES):
        for c in range(C // LANES):
            tokens[j * FRAMES : (j + 1) * FRAMES, c * LANES : (c + 1) * LANES] = rows[
                pl.ds(j * 5 + c, FRAMES, stride=SENT + 1), :
            ].astype(bf16)
    projected = dot_t(tokens[...], weight[...])
    query = (projected[:, C:] * QUERY_SCALE).astype(bf16)
    query = jnp.concatenate([query, jnp.zeros((CELLS, 64), bf16)], axis=1)
    kv = projected[:, 0:C].astype(bf16)
    span = 3 * FRAMES
    row_place = lax.broadcasted_iota(jnp.int32, (span, span), 0) // FRAMES
    column_place = lax.broadcasted_iota(jnp.int32, (span, span), 1) // FRAMES
    same = row_place == column_place
    for first in range(0, CELLS, span):
        gathered = []
        for h in range(HEADS):
            key_low, key_high = KEY_WINDOW[h]
            low, high = VALUE_WINDOW[h]
            scores = dot_t(
                head_query(query[first : first + span], h),
                kv[first : first + span, key_low:key_high],
            )
            weights = jnp.where(same, jnp.exp2(scores), 0.0).astype(bf16)
            values = jnp.where(
                inside_value(h), kv[first : first + span, low:high], jnp.ones((), bf16)
            )
            gathered.append(dot(weights, values))
        blocks = normalised(gathered)
        for b in range(3):
            result[first : first + span, b * LANES : (b + 1) * LANES] = blocks[b]
    for j in range(PLACES):
        cell = slice(j * FRAMES, (j + 1) * FRAMES)
        for b in range(2):
            rows[pl.ds(j * 2 + b, FRAMES, stride=BACK + 1), :] = result[
                cell, (1 + b) * LANES : (2 + b) * LANES
            ]
    for pair in range((PLACES + 1) // 2):
        half = result[2 * pair * FRAMES : (2 * pair + 1) * FRAMES, 0:LANES]
        if 2 * pair + 1 < PLACES:
            other = result[(2 * pair + 1) * FRAMES : (2 * pair + 2) * FRAMES, 0:LANES]
            half = half + pltpu.roll(other, LANES // 2, 1)
        rows[pl.ds(2 * PLACES + pair, FRAMES, stride=BACK + 1), :] = half
    rows[pl.ds(BACK - 1, FRAMES, stride=BACK + 1), :] = jnp.zeros((FRAMES, LANES), f32)
    for g in range(FRAMES):
        out_ref[g * BACK : (g + 1) * BACK, :] = rows[
            g * (BACK + 1) : g * (BACK + 1) + BACK, :
        ].astype(bf16)


def final_kernel(got_ref, weight_ref, mixed_ref, out_ref, rows, attended, weight):
    weight[0:64, :] = jnp.zeros((64, C), bf16)
    weight[64:, :] = weight_ref[...]
    for g in range(FRAMES):
        rows[g * (BACK + 1) : g * (BACK + 1) + BACK, :] = got_ref[
            g * BACK : (g + 1) * BACK, :
        ].astype(f32)
    upper = lane_iota(LANES) >= LANES // 2
    for j in range(PLACES):
        cell = slice(j * FRAMES, (j + 1) * FRAMES)
        for b in range(2):
            attended[cell, (1 + b) * LANES : (2 + b) * LANES] = rows[
                pl.ds(j * 2 + b, FRAMES, stride=BACK + 1), :
            ].astype(bf16)
        half = rows[pl.ds(2 * PLACES + j // 2, FRAMES, stride=BACK + 1), :]
        if j % 2:
            half = pltpu.roll(half, LANES // 2, 1)
        attended[cell, 0:LANES] = jnp.where(upper, half, 0.0).astype(bf16)
    update = dot(attended[...], weight[...])
    out_ref[...] = (mixed_ref[...].astype(f32) + update).astype(bf16)


def order_kernel(value_ref, before_ref, out_ref):
    pass


def after(value, before):
    return pl.pallas_call(
        order_kernel,
        out_shape=struct(value.shape, value.dtype),
        in_specs=[pl.BlockSpec(memory_space=pl.ANY)] * 2,
        out_specs=pl.BlockSpec(memory_space=pl.ANY),
        input_output_aliases={0: 0},
        compiler_params=pltpu.CompilerParams(vmem_limit_bytes=1 << 20),
        cost_estimate=pl.CostEstimate(flops=0, bytes_accessed=0, transcendentals=0),
    )(value, before)


def struct(shape, dtype):
    return jax.ShapeDtypeStruct(shape, dtype)


def on_device(
    latent,
    reference_states,
    group_gain,
    conv_weight,
    norm_gain,
    spatial_query,
    spatial_key,
    spatial_value,
    spatial_out,
    frame_gain,
    temporal_query,
    temporal_key,
    temporal_value,
    temporal_out,
):
    x = latent.reshape(CELLS, C)
    strip_at = lax.axis_index("space")
    odd_row = lax.axis_index("frame") // 8 % 2 == 1
    flags = (
        jnp.stack([strip_at > 0, strip_at < 3, strip_at % 2 == 1, odd_row])
        .astype(f32)
        .reshape(1, 4)
    )

    def swap(value, k):
        return lax.ppermute(value, "space", [(i, i ^ k) for i in range(4)])

    states = reference_states.reshape(CELLS, C)
    sums, near, edge = call(
        stats_kernel,
        [struct((8, C), f32), struct((W + 16, C), bf16), struct((W, C), bf16)],
        [flags, x],
        smem=1,
        flops=2 * 10**9,
    )
    near = swap(near, 1)
    sums, far = call(
        chip_sums_kernel,
        [struct((8, C), f32), struct((W + 16, C), bf16)],
        [sums, near, edge],
        flops=2 * 10**9,
    )
    far = swap(far, 3)

    ref_kv, half = call(
        reference_kernel,
        [struct((CELLS, C), bf16), struct((CELLS // 2, C), bf16)],
        [flags, states, sums, spatial_key.T, spatial_value.T],
        scratch=[pltpu.VMEM((C, C), bf16)],
        smem=1,
        flops=2 * 10**9,
        limit=8,
    )
    half = swap(half, 2)

    hidden, query, kv, low, high, first, second = call(
        conv_kernel,
        [
            struct((CELLS, C), bf16),
            struct((CELLS, 384), bf16),
            struct((CELLS, C), bf16),
            struct((PART, C), bf16),
            struct((PART, C), bf16),
            struct((FIRST, C), bf16),
            struct((CELLS - FIRST, C), bf16),
        ],
        [
            flags,
            sums,
            x,
            near,
            far,
            group_gain,
            conv_weight.reshape(3, 3 * C, C),
            norm_gain,
            spatial_query.T,
            spatial_key.T,
            spatial_value.T,
        ],
        scratch=[
            pltpu.VMEM(((STRIP + 2) * W, 3 * C), bf16),
            pltpu.VMEM((C + INNER, C), bf16),
        ],
        smem=1,
        limit=16,
    )

    ref_near = swap(ref_kv, 1)
    half = after(half, query)
    other_half = lax.ppermute(half, "frame", [(f, f ^ 8) for f in range(FRAMES)])
    half_near = swap(half, 1)
    first = swap(first, 2)
    second = swap(second, 2)
    kv_near = [swap(low, 1), swap(high, 1)]

    def attention(kv_parts, start):
        ranges = [(low, high) for _, low, high in kv_parts]
        keys = sum(high - low for low, high in ranges)
        return call(
            functools.partial(attention_kernel, ranges, start is not None),
            struct((CELLS, ACC_WIDTH), f32),
            [query, *(part for part, _, _ in kv_parts)] + ([] if start is None else [start]),
            scratch=[pltpu.VMEM((keys, C), bf16)],
            limit=16,
        )

    acc = attention(
        [(part, 0, part.shape[0]) for part in (kv, *kv_near, ref_kv, ref_near, half)]
        + [(half_near, 0, EARLY)],
        None,
    )
    sizes = (PART // 2, PART // 2, FIRST // 2, FIRST // 2)
    parts = call(
        parts_kernel,
        [struct((size, C), bf16) for size in sizes],
        [other_half, first, acc],
        anywhere=(2,),
    )
    near_parts = [swap(part, 1) for part in parts]
    acc = attention(
        [(half_near, EARLY, PART), (parts[0], 0, PART // 2), (parts[1], 0, HEAD)], acc
    )
    rest = [parts[1], *near_parts[:2], *parts[2:], *near_parts[2:]]
    acc = attention([(part, HEAD if i == 0 else 0, part.shape[0]) for i, part in enumerate(rest)], acc)
    second = after(second, acc)
    second_near = swap(second, 1)
    acc = attention([(second, 0, CELLS - FIRST)], acc)
    mixed, sent = call(
        last_attention_kernel,
        [struct((CELLS, C), bf16), struct((FRAMES * SENT, LANES), bf16)],
        [query, acc, second_near, hidden, spatial_out, frame_gain],
        scratch=[
            pltpu.VMEM((FRAMES * (SENT + 1), LANES), f32),
            pltpu.VMEM((384, C), bf16),
        ],
        limit=16,
    )
    got = lax.all_to_all(
        sent.reshape(FRAMES, SENT, LANES), "frame", split_axis=0, concat_axis=0, tiled=True
    )
    back = call(
        temporal_kernel,
        struct((FRAMES * BACK, LANES), bf16),
        [
            got.reshape(FRAMES * SENT, LANES),
            temporal_query.T,
            temporal_key.T,
            temporal_value.T,
        ],
        scratch=[
            pltpu.VMEM((FRAMES * (SENT + 1), LANES), f32),
            pltpu.VMEM((CELLS, C), bf16),
            pltpu.VMEM((CELLS, 384), f32),
            pltpu.VMEM((C + INNER, C), bf16),
        ],
    )
    returned = lax.all_to_all(
        back.reshape(FRAMES, BACK, LANES), "frame", split_axis=0, concat_axis=0, tiled=True
    )
    output = call(
        final_kernel,
        struct((CELLS, C), bf16),
        [returned.reshape(FRAMES * BACK, LANES), temporal_out, mixed],
        scratch=[
            pltpu.VMEM((FRAMES * (BACK + 1), LANES), f32),
            pltpu.VMEM((CELLS, 384), bf16),
            pltpu.VMEM((384, C), bf16),
        ],
    )
    return output.reshape(latent.shape)


def solution(mesh):
    return jax.shard_map(
        on_device,
        mesh=mesh,
        in_specs=(P("frame", "space", None, None), P("space", None, None)) + (P(),) * 12,
        out_specs=P("frame", "space", None, None),
        check_vma=False,
    )
```

```python
import functools

import jax
import jax.numpy as jnp
from jax import lax
from jax.experimental import pallas as pl
from jax.experimental.pallas import tpu as pltpu
from jax.sharding import PartitionSpec as P

HEADS = 4
HEAD_DIM = 80
GROUPS = 32
INNER = 320
C = 640
W = 48
STRIP = 12
CELLS = STRIP * W
FRAMES = 64
PLACES = CELLS // FRAMES
LANES = 128
SENT = 48
TILE = 768
EARLY = 224
HEAD = 48
FIRST = 320
PART = CELLS // 2
BACK = 24

epsilon = 1e-05
QUERY_SCALE = HEAD_DIM**-0.5 * 1.4426950408889634

KEY_WINDOW = ((0, 128), (0, 256), (128, 256), (128, 384))
VALUE_WINDOW = ((256, 512), (384, 512), (384, 640), (512, 640))
ACC_AT = (0, 256, 384, 640)
ACC_WIDTH = 768

ORDER = [(x * 4 + y) * 8 + z for z in range(8) for x in range(2) for y in range(4)]

f32 = jnp.float32
bf16 = jnp.bfloat16


def lane_iota(width, start=0):
    return lax.broadcasted_iota(jnp.int32, (1, width), 1) + start


def layer_norm(values, factor):
    centre = jnp.mean(values, axis=-1, keepdims=True)
    shifted = values - centre
    spread = jnp.mean(shifted * shifted, axis=-1, keepdims=True)
    normed = shifted * lax.rsqrt(spread + epsilon)
    return normed if factor is None else normed * factor


def dot(a, b):
    return jnp.dot(a, b, preferred_element_type=f32)


def dot_t(a, b):
    return lax.dot_general(a, b, (((1,), (1,)), ((), ())), preferred_element_type=f32)


def vmem(count):
    return [pl.BlockSpec(memory_space=pltpu.VMEM)] * count


def call(
    body, outs, operands, scratch=(), smem=0, limit=8, anywhere=(), flops=0, out_anywhere=False
):
    single = not isinstance(outs, (list, tuple))
    specs = [pl.BlockSpec(memory_space=pltpu.SMEM)] * smem + vmem(len(operands) - smem)
    for i in anywhere:
        specs[i] = pl.BlockSpec(memory_space=pl.ANY)
    return pl.pallas_call(
        body,
        out_shape=outs,
        in_specs=specs,
        out_specs=pl.BlockSpec(memory_space=pl.ANY)
        if out_anywhere
        else vmem(1)[0]
        if single
        else vmem(len(outs)),
        scratch_shapes=list(scratch),
        compiler_params=pltpu.CompilerParams(vmem_limit_bytes=limit * 1024 * 1024),
        cost_estimate=pl.CostEstimate(flops=flops, bytes_accessed=0, transcendentals=0),
    )(*operands)


def pieces_of(value):
    high = value.astype(bf16).astype(f32)
    middle = (value - high).astype(bf16).astype(f32)
    return [high, middle, value - high - middle]


def stacked(rows, height):
    at = lax.broadcasted_iota(jnp.int32, (height, C), 0)
    result = jnp.zeros((height, C), f32)
    for i, row in enumerate(rows):
        result = jnp.where(at == i, row, result)
    return result


def sums_of(pieces):
    return pieces[0:1] + pieces[1:2] + pieces[2:3], pieces[3:4] + pieces[4:5] + pieces[5:6]


def stats_kernel(flags_ref, x_ref, sums_ref, near_ref, far_ref):
    total = jnp.zeros((1, C), f32)
    square = jnp.zeros((1, C), f32)
    for r in range(STRIP):
        v = x_ref[r * W : (r + 1) * W, :].astype(f32)
        total = total + jnp.sum(v, axis=0, keepdims=True)
        square = square + jnp.sum(v * v, axis=0, keepdims=True)
    per = C // GROUPS
    column_group = jnp.floor((lane_iota(C).astype(f32) + 0.5) * (1.0 / per))
    row_at = lax.broadcasted_iota(jnp.int32, (C, 1), 0).astype(f32)
    row_group = jnp.floor((row_at + 0.5) * (1.0 / per))
    same = jnp.where(row_group == column_group, 1.0, 0.0).astype(bf16)
    grouped = dot(stacked(pieces_of(total) + pieces_of(square), 16).astype(bf16), same)
    group_sum, group_sq = sums_of(grouped)
    sums_ref[...] = stacked([group_sum, group_sq], 8)
    near_ref[W:, :] = stacked(pieces_of(group_sum) + pieces_of(group_sq), 16).astype(bf16)
    odd = flags_ref[0, 2] > 0.5
    top = x_ref[0:W, :]
    bottom = x_ref[CELLS - W :, :]
    near_ref[0:W, :] = jnp.where(odd, top, bottom)
    far_ref[...] = jnp.where(odd, bottom, top)


def chip_sums_kernel(sums_ref, near_ref, edge_ref, sums_out, far_ref):
    group_sum, group_sq = sums_of(near_ref[W:, :].astype(f32))
    group_sum = group_sum + sums_ref[0:1]
    group_sq = group_sq + sums_ref[1:2]
    sums_out[...] = stacked([group_sum, group_sq], 8)
    far_ref[0:W, :] = edge_ref[...]
    far_ref[W:, :] = stacked(pieces_of(group_sum) + pieces_of(group_sq), 16).astype(bf16)


def reference_kv(weight, states):
    normed = layer_norm(states.astype(f32), None).astype(bf16)
    return dot_t(normed, weight[...]).astype(bf16)


def reference_kernel(
    flags_ref, states_ref, before_ref, key_ref, value_ref, out_ref, half_ref, weight
):
    weight[0:INNER, :] = key_ref[...]
    weight[INNER:, :] = value_ref[...]
    out_ref[...] = reference_kv(weight, states_ref[...])
    half_ref[...] = jnp.where(flags_ref[0, 3] > 0.5, out_ref[PART:, :], out_ref[0:PART, :])


def parts_kernel(first_ref, second_ref, before_ref, *part_refs):
    for i, part_ref in enumerate(part_refs):
        ref = (first_ref, second_ref)[i // 2]
        size = part_ref.shape[0]
        part_ref[...] = ref[i % 2 * size : (i % 2 + 1) * size, :]


def joined_weights(weight, key_ref, value_ref, query_ref):
    weight[0:INNER, :] = key_ref[...]
    weight[INNER:C, :] = value_ref[...]
    weight[C:, :] = query_ref[...]


def conv_kernel(
    flags_ref,
    sums_ref,
    x_ref,
    near_ref,
    far_ref,
    gain_ref,
    kernel_ref,
    norm_gain_ref,
    query_ref,
    key_ref,
    value_ref,
    hidden_out,
    query_out,
    kv_out,
    low_out,
    high_out,
    first_out,
    second_out,
    lhs,
    weight,
):
    joined_weights(weight, key_ref, value_ref, query_ref)
    group_sum, group_sq = sums_of(far_ref[W:, :].astype(f32))
    members = float(4 * CELLS * (C // GROUPS))
    average = (group_sum + sums_ref[0:1]) / members
    variance = (group_sq + sums_ref[1:2]) / members - average * average
    factor = lax.rsqrt(variance + epsilon) * gain_ref[...].reshape(1, C)
    at = lax.broadcasted_iota(jnp.int32, (W, 1), 0)
    odd = flags_ref[0, 2] > 0.5

    def place(r, block, keep):
        v = (block.astype(f32) - average) * factor
        act = (0.5 * v) * (1.0 + jnp.tanh(0.5 * v))
        if keep is not None:
            act = jnp.where(keep > 0.5, act, 0.0)
        rows = slice(r * W, (r + 1) * W)
        lhs[rows, C : 2 * C] = act.astype(bf16)
        lhs[rows, 0:C] = jnp.where(at == 0, 0.0, pltpu.roll(act, 1, 0)).astype(bf16)
        lhs[rows, 2 * C :] = jnp.where(at == W - 1, 0.0, pltpu.roll(act, W - 1, 0)).astype(bf16)

    near, far = near_ref[0:W, :], far_ref[0:W, :]
    place(0, jnp.where(odd, near, far), flags_ref[0, 0])
    place(STRIP + 1, jnp.where(odd, far, near), flags_ref[0, 1])
    for r in range(STRIP):
        place(r + 1, x_ref[r * W : (r + 1) * W, :], None)
    for first in (0, CELLS // 2):
        rows = slice(first, first + CELLS // 2)
        total = None
        for a in range(3):
            part = dot(lhs[first + a * W : first + a * W + CELLS // 2, :], kernel_ref[a])
            total = part if total is None else total + part
        hidden_out[rows, :] = (x_ref[rows, :].astype(f32) + total).astype(bf16)
    normed = layer_norm(hidden_out[...].astype(f32), norm_gain_ref[...].reshape(1, C)).astype(bf16)
    projected = dot_t(normed, weight[...])
    kv = projected[:, 0:C].astype(bf16)
    kv_out[...] = kv
    low_out[...] = kv[0:PART]
    high_out[...] = kv[PART:]
    first_out[...] = kv[0:FIRST]
    second_out[...] = kv[FIRST:]
    query_out[:, 0:INNER] = (projected[:, C:] * QUERY_SCALE).astype(bf16)
    query_out[:, INNER:] = jnp.zeros((CELLS, 64), bf16)


def head_query(query, h):
    low, high = KEY_WINDOW[h]
    lane = lane_iota(high - low, low)
    inside = (lane >= h * HEAD_DIM) & (lane < (h + 1) * HEAD_DIM)
    return jnp.where(inside, query[:, low:high], jnp.zeros((), bf16))


def inside_value(h):
    low, high = VALUE_WINDOW[h]
    lane = lane_iota(high - low, low)
    return (lane >= INNER + h * HEAD_DIM) & (lane < INNER + (h + 1) * HEAD_DIM)


def joined(kv_refs, ranges, scratch):
    at = 0
    for ref, (low, high) in zip(kv_refs, ranges):
        scratch[at : at + high - low, :] = ref[low:high, :]
        at += high - low
    return scratch


def attend(query, kv_ref, start):
    gathered = []
    keys = kv_ref.shape[0]
    for h in range(HEADS):
        key_low, key_high = KEY_WINDOW[h]
        low, high = VALUE_WINDOW[h]
        mine = head_query(query, h)
        inside = inside_value(h)
        acc = None if start is None else start(h)
        for first in range(0, keys, TILE):
            rows = slice(first, min(first + TILE, keys))
            weights = jnp.exp2(dot_t(mine, kv_ref[rows, key_low:key_high])).astype(bf16)
            values = jnp.where(inside, kv_ref[rows, low:high], jnp.ones((), bf16))
            part = dot(weights, values)
            acc = part if acc is None else acc + part
        gathered.append(acc)
    return gathered


def normalised(gathered):
    blocks = [None, None, None]
    for h in range(HEADS):
        low, high = VALUE_WINDOW[h]
        acc = gathered[h]
        spare = 0 if INNER + h * HEAD_DIM > low else high - low - 1
        result = acc * (1.0 / acc[:, spare : spare + 1])
        result = jnp.where(inside_value(h), result, 0.0)
        for b in range((high - low) // LANES):
            at = low // LANES + b - 2
            piece = result[:, b * LANES : (b + 1) * LANES]
            blocks[at] = piece if blocks[at] is None else blocks[at] + piece
    return blocks


def starting(acc_ref):
    return lambda h: acc_ref[:, ACC_AT[h] : ACC_AT[h] + VALUE_WINDOW[h][1] - VALUE_WINDOW[h][0]]


def attention_kernel(ranges, has_start, *refs):
    n_kv = len(ranges)
    query_ref = refs[0]
    start = starting(refs[1 + n_kv]) if has_start else None
    out_ref, scratch = refs[-2:]
    kv_ref = joined(refs[1 : 1 + n_kv], ranges, scratch)
    for h, acc in enumerate(attend(query_ref[...], kv_ref, start)):
        out_ref[:, ACC_AT[h] : ACC_AT[h] + acc.shape[1]] = acc


def last_attention_kernel(
    query_ref,
    acc_ref,
    kv_ref,
    hidden_ref,
    weight_ref,
    gain_ref,
    mixed_out,
    sent_out,
    rows,
    weight,
):
    weight[0:64, :] = jnp.zeros((64, C), bf16)
    weight[64:, :] = weight_ref[...]
    blocks = normalised(attend(query_ref[...], kv_ref, starting(acc_ref)))
    attended = jnp.concatenate([block.astype(bf16) for block in blocks], axis=1)
    update = dot(attended, weight[...])
    mixed = (hidden_ref[...].astype(f32) + update).astype(bf16)
    mixed_out[...] = mixed
    framed = layer_norm(mixed.astype(f32), gain_ref[...].reshape(1, C))
    for j in range(PLACES):
        for c in range(C // LANES):
            rows[pl.ds(j * 5 + c, FRAMES, stride=SENT + 1), :] = framed[
                j * FRAMES : (j + 1) * FRAMES, c * LANES : (c + 1) * LANES
            ]
    for r in range(PLACES * 5, SENT):
        rows[pl.ds(r, FRAMES, stride=SENT + 1), :] = jnp.zeros((FRAMES, LANES), f32)
    for g in range(FRAMES):
        sent_out[g * SENT : (g + 1) * SENT, :] = rows[
            g * (SENT + 1) : g * (SENT + 1) + SENT, :
        ].astype(bf16)


def temporal_kernel(
    got_ref, query_ref, key_ref, value_ref, out_ref, rows, tokens, result, weight
):
    joined_weights(weight, key_ref, value_ref, query_ref)
    for g in range(FRAMES):
        rows[g * (SENT + 1) : g * (SENT + 1) + SENT, :] = got_ref[
            g * SENT : (g + 1) * SENT, :
        ].astype(f32)
    for j in range(PLACES):
        for c in range(C // LANES):
            tokens[j * FRAMES : (j + 1) * FRAMES, c * LANES : (c + 1) * LANES] = rows[
                pl.ds(j * 5 + c, FRAMES, stride=SENT + 1), :
            ].astype(bf16)
    projected = dot_t(tokens[...], weight[...])
    query = (projected[:, C:] * QUERY_SCALE).astype(bf16)
    query = jnp.concatenate([query, jnp.zeros((CELLS, 64), bf16)], axis=1)
    kv = projected[:, 0:C].astype(bf16)
    span = 3 * FRAMES
    row_place = lax.broadcasted_iota(jnp.int32, (span, span), 0) // FRAMES
    column_place = lax.broadcasted_iota(jnp.int32, (span, span), 1) // FRAMES
    same = row_place == column_place
    for first in range(0, CELLS, span):
        gathered = []
        for h in range(HEADS):
            key_low, key_high = KEY_WINDOW[h]
            low, high = VALUE_WINDOW[h]
            scores = dot_t(
                head_query(query[first : first + span], h),
                kv[first : first + span, key_low:key_high],
            )
            weights = jnp.where(same, jnp.exp2(scores), 0.0).astype(bf16)
            values = jnp.where(
                inside_value(h), kv[first : first + span, low:high], jnp.ones((), bf16)
            )
            gathered.append(dot(weights, values))
        blocks = normalised(gathered)
        for b in range(3):
            result[first : first + span, b * LANES : (b + 1) * LANES] = blocks[b]
    for j in range(PLACES):
        cell = slice(j * FRAMES, (j + 1) * FRAMES)
        for b in range(2):
            rows[pl.ds(j * 2 + b, FRAMES, stride=BACK + 1), :] = result[
                cell, (1 + b) * LANES : (2 + b) * LANES
            ]
    for pair in range((PLACES + 1) // 2):
        half = result[2 * pair * FRAMES : (2 * pair + 1) * FRAMES, 0:LANES]
        if 2 * pair + 1 < PLACES:
            other = result[(2 * pair + 1) * FRAMES : (2 * pair + 2) * FRAMES, 0:LANES]
            half = half + pltpu.roll(other, LANES // 2, 1)
        rows[pl.ds(2 * PLACES + pair, FRAMES, stride=BACK + 1), :] = half
    rows[pl.ds(BACK - 1, FRAMES, stride=BACK + 1), :] = jnp.zeros((FRAMES, LANES), f32)
    for g in range(0, FRAMES, 2):
        pair = [rows[i * (BACK + 1) : i * (BACK + 1) + BACK, :] for i in (g, g + 1)]
        out_ref[g * BACK : (g + 2) * BACK, :] = jnp.concatenate(pair, axis=0).astype(bf16)


def final_kernel(got_ref, weight_ref, mixed_ref, out_ref, rows, attended, weight, staged, left):
    weight[0:64, :] = jnp.zeros((64, C), bf16)
    weight[64:, :] = weight_ref[...]
    for g in range(0, FRAMES, 2):
        pair = got_ref[g * BACK : (g + 2) * BACK, :].astype(f32)
        for i in range(2):
            rows[(g + i) * (BACK + 1) : (g + i) * (BACK + 1) + BACK, :] = pair[
                i * BACK : (i + 1) * BACK, :
            ]
    upper = lane_iota(LANES) >= LANES // 2
    parts = 3
    copies = []
    for part in range(parts):
        for j in range(part * PLACES // parts, (part + 1) * PLACES // parts):
            cell = slice(j * FRAMES, (j + 1) * FRAMES)
            for b in range(2):
                attended[cell, (1 + b) * LANES : (2 + b) * LANES] = rows[
                    pl.ds(j * 2 + b, FRAMES, stride=BACK + 1), :
                ].astype(bf16)
            half = rows[pl.ds(2 * PLACES + j // 2, FRAMES, stride=BACK + 1), :]
            if j % 2:
                half = pltpu.roll(half, LANES // 2, 1)
            attended[cell, 0:LANES] = jnp.where(upper, half, 0.0).astype(bf16)
        size = CELLS // parts
        cells = slice(part * size, (part + 1) * size)
        update = dot(attended[cells, :], weight[...])
        staged[cells, :] = (mixed_ref[cells, :].astype(f32) + update).astype(bf16)
        at = pl.ds(part * size, size)
        copies.append(pltpu.make_async_copy(staged.at[at], out_ref.at[at], left.at[part]))
        copies[-1].start()
    for copy in copies:
        copy.wait()


def order_kernel(value_ref, before_ref, out_ref):
    pass


def after(value, before):
    return pl.pallas_call(
        order_kernel,
        out_shape=struct(value.shape, value.dtype),
        in_specs=[pl.BlockSpec(memory_space=pl.ANY)] * 2,
        out_specs=pl.BlockSpec(memory_space=pl.ANY),
        input_output_aliases={0: 0},
        compiler_params=pltpu.CompilerParams(vmem_limit_bytes=1 << 20),
        cost_estimate=pl.CostEstimate(flops=0, bytes_accessed=0, transcendentals=0),
    )(value, before)


def struct(shape, dtype):
    return jax.ShapeDtypeStruct(shape, dtype)


def on_device(
    latent,
    reference_states,
    group_gain,
    conv_weight,
    norm_gain,
    spatial_query,
    spatial_key,
    spatial_value,
    spatial_out,
    frame_gain,
    temporal_query,
    temporal_key,
    temporal_value,
    temporal_out,
):
    x = latent.reshape(CELLS, C)
    strip_at = lax.axis_index("space")
    odd_row = lax.axis_index("frame") // 8 % 2 == 1
    flags = (
        jnp.stack([strip_at > 0, strip_at < 3, strip_at % 2 == 1, odd_row])
        .astype(f32)
        .reshape(1, 4)
    )

    def swap(value, k):
        return lax.ppermute(value, "space", [(i, i ^ k) for i in range(4)])

    states = reference_states.reshape(CELLS, C)
    sums, near, edge = call(
        stats_kernel,
        [struct((8, C), f32), struct((W + 16, C), bf16), struct((W, C), bf16)],
        [flags, x],
        smem=1,
        flops=2 * 10**9,
    )
    near = swap(near, 1)
    sums, far = call(
        chip_sums_kernel,
        [struct((8, C), f32), struct((W + 16, C), bf16)],
        [sums, near, edge],
        flops=2 * 10**9,
    )
    far = swap(far, 3)

    ref_kv, half = call(
        reference_kernel,
        [struct((CELLS, C), bf16), struct((CELLS // 2, C), bf16)],
        [flags, states, sums, spatial_key.T, spatial_value.T],
        scratch=[pltpu.VMEM((C, C), bf16)],
        smem=1,
        flops=2 * 10**9,
        limit=8,
    )
    half = swap(half, 2)

    hidden, query, kv, low, high, first, second = call(
        conv_kernel,
        [
            struct((CELLS, C), bf16),
            struct((CELLS, 384), bf16),
            struct((CELLS, C), bf16),
            struct((PART, C), bf16),
            struct((PART, C), bf16),
            struct((FIRST, C), bf16),
            struct((CELLS - FIRST, C), bf16),
        ],
        [
            flags,
            sums,
            x,
            near,
            far,
            group_gain,
            conv_weight.reshape(3, 3 * C, C),
            norm_gain,
            spatial_query.T,
            spatial_key.T,
            spatial_value.T,
        ],
        scratch=[
            pltpu.VMEM(((STRIP + 2) * W, 3 * C), bf16),
            pltpu.VMEM((C + INNER, C), bf16),
        ],
        smem=1,
        limit=16,
    )

    ref_near = swap(ref_kv, 1)
    half = after(half, query)
    other_half = lax.ppermute(half, "frame", [(f, f ^ 8) for f in range(FRAMES)])
    half_near = swap(half, 1)
    first = swap(first, 2)
    second = swap(second, 2)
    kv_near = [swap(low, 1), swap(high, 1)]

    def attention(kv_parts, start):
        ranges = [(low, high) for _, low, high in kv_parts]
        keys = sum(high - low for low, high in ranges)
        return call(
            functools.partial(attention_kernel, ranges, start is not None),
            struct((CELLS, ACC_WIDTH), f32),
            [query, *(part for part, _, _ in kv_parts)] + ([] if start is None else [start]),
            scratch=[pltpu.VMEM((keys, C), bf16)],
            limit=16,
        )

    acc = attention(
        [(part, 0, part.shape[0]) for part in (kv, *kv_near, ref_kv, ref_near, half)]
        + [(half_near, 0, EARLY)],
        None,
    )
    sizes = (PART // 2, PART // 2, FIRST // 2, FIRST // 2)
    parts = call(
        parts_kernel,
        [struct((size, C), bf16) for size in sizes],
        [other_half, first, acc],
        anywhere=(2,),
    )
    near_parts = [swap(part, 1) for part in parts]
    acc = attention(
        [(half_near, EARLY, PART), (parts[0], 0, PART // 2), (parts[1], 0, HEAD)], acc
    )
    rest = [parts[1], *near_parts[:2], *parts[2:], *near_parts[2:]]
    acc = attention([(part, HEAD if i == 0 else 0, part.shape[0]) for i, part in enumerate(rest)], acc)
    second = after(second, acc)
    second_near = swap(second, 1)
    acc = attention([(second, 0, CELLS - FIRST)], acc)
    mixed, sent = call(
        last_attention_kernel,
        [struct((CELLS, C), bf16), struct((FRAMES * SENT, LANES), bf16)],
        [query, acc, second_near, hidden, spatial_out, frame_gain],
        scratch=[
            pltpu.VMEM((FRAMES * (SENT + 1), LANES), f32),
            pltpu.VMEM((384, C), bf16),
        ],
        limit=16,
    )
    got = lax.all_to_all(
        sent.reshape(FRAMES, SENT, LANES), "frame", split_axis=0, concat_axis=0, axis_index_groups=[ORDER], tiled=True
    )
    back = call(
        temporal_kernel,
        struct((FRAMES * BACK, LANES), bf16),
        [
            got.reshape(FRAMES * SENT, LANES),
            temporal_query.T,
            temporal_key.T,
            temporal_value.T,
        ],
        scratch=[
            pltpu.VMEM((FRAMES * (SENT + 1), LANES), f32),
            pltpu.VMEM((CELLS, C), bf16),
            pltpu.VMEM((CELLS, 384), f32),
            pltpu.VMEM((C + INNER, C), bf16),
        ],
    )
    returned = lax.all_to_all(
        back.reshape(FRAMES, BACK, LANES), "frame", split_axis=0, concat_axis=0, axis_index_groups=[ORDER], tiled=True
    )
    output = call(
        final_kernel,
        struct((CELLS, C), bf16),
        [returned.reshape(FRAMES * BACK, LANES), temporal_out, mixed],
        scratch=[
            pltpu.VMEM((FRAMES * (BACK + 1), LANES), f32),
            pltpu.VMEM((CELLS, 384), bf16),
            pltpu.VMEM((384, C), bf16),
            pltpu.VMEM((CELLS, C), bf16),
            pltpu.SemaphoreType.DMA((3,)),
        ],
        out_anywhere=True,
    )
    return output.reshape(latent.shape)


def solution(mesh):
    return jax.shard_map(
        on_device,
        mesh=mesh,
        in_specs=(P("frame", "space", None, None), P("space", None, None)) + (P(),) * 12,
        out_specs=P("frame", "space", None, None),
        check_vma=False,
    )
```

```python
import functools

import jax
import jax.numpy as jnp
from jax import lax
from jax.experimental import pallas as pl
from jax.experimental.pallas import tpu as pltpu
from jax.sharding import PartitionSpec as P

HEADS = 4
HEAD_DIM = 80
GROUPS = 32
INNER = 320
C = 640
W = 48
STRIP = 12
CELLS = STRIP * W
FRAMES = 64
PLACES = CELLS // FRAMES
LANES = 128
SENT = 48
WHOLE = 256
TILE = 768
EARLY = 224
HEAD = 48
FIRST = 320
PART = CELLS // 2
BACK = 24

epsilon = 1e-05
QUERY_SCALE = HEAD_DIM**-0.5 * 1.4426950408889634

KEY_WINDOW = ((0, 128), (0, 256), (128, 256), (128, 384))
VALUE_WINDOW = ((256, 512), (384, 512), (384, 640), (512, 640))
ACC_AT = (0, 256, 384, 640)
ACC_WIDTH = 768

ORDER = [(x * 4 + y) * 8 + z for z in range(8) for y in range(4) for x in range(2)]

f32 = jnp.float32
bf16 = jnp.bfloat16


def lane_iota(width, start=0):
    return lax.broadcasted_iota(jnp.int32, (1, width), 1) + start


def layer_norm(values, factor):
    centre = jnp.mean(values, axis=-1, keepdims=True)
    shifted = values - centre
    spread = jnp.mean(shifted * shifted, axis=-1, keepdims=True)
    normed = shifted * lax.rsqrt(spread + epsilon)
    return normed if factor is None else normed * factor


def dot(a, b):
    return jnp.dot(a, b, preferred_element_type=f32)


def dot_t(a, b):
    return lax.dot_general(a, b, (((1,), (1,)), ((), ())), preferred_element_type=f32)


def vmem(count):
    return [pl.BlockSpec(memory_space=pltpu.VMEM)] * count


def call(
    body, outs, operands, scratch=(), smem=0, limit=8, anywhere=(), flops=0, out_anywhere=False
):
    single = not isinstance(outs, (list, tuple))
    specs = [pl.BlockSpec(memory_space=pltpu.SMEM)] * smem + vmem(len(operands) - smem)
    for i in anywhere:
        specs[i] = pl.BlockSpec(memory_space=pl.ANY)
    return pl.pallas_call(
        body,
        out_shape=outs,
        in_specs=specs,
        out_specs=pl.BlockSpec(memory_space=pl.ANY)
        if out_anywhere
        else vmem(1)[0]
        if single
        else vmem(len(outs)),
        scratch_shapes=list(scratch),
        compiler_params=pltpu.CompilerParams(vmem_limit_bytes=limit * 1024 * 1024),
        cost_estimate=pl.CostEstimate(flops=flops, bytes_accessed=0, transcendentals=0),
    )(*operands)


def pieces_of(value):
    high = value.astype(bf16).astype(f32)
    middle = (value - high).astype(bf16).astype(f32)
    return [high, middle, value - high - middle]


def stacked(rows, height):
    at = lax.broadcasted_iota(jnp.int32, (height, C), 0)
    result = jnp.zeros((height, C), f32)
    for i, row in enumerate(rows):
        result = jnp.where(at == i, row, result)
    return result


def sums_of(pieces):
    return pieces[0:1] + pieces[1:2] + pieces[2:3], pieces[3:4] + pieces[4:5] + pieces[5:6]


def stats_kernel(flags_ref, x_ref, sums_ref, near_ref, far_ref):
    total = jnp.zeros((1, C), f32)
    square = jnp.zeros((1, C), f32)
    for r in range(STRIP):
        v = x_ref[r * W : (r + 1) * W, :].astype(f32)
        total = total + jnp.sum(v, axis=0, keepdims=True)
        square = square + jnp.sum(v * v, axis=0, keepdims=True)
    per = C // GROUPS
    column_group = jnp.floor((lane_iota(C).astype(f32) + 0.5) * (1.0 / per))
    row_at = lax.broadcasted_iota(jnp.int32, (C, 1), 0).astype(f32)
    row_group = jnp.floor((row_at + 0.5) * (1.0 / per))
    same = jnp.where(row_group == column_group, 1.0, 0.0).astype(bf16)
    grouped = dot(stacked(pieces_of(total) + pieces_of(square), 16).astype(bf16), same)
    group_sum, group_sq = sums_of(grouped)
    sums_ref[...] = stacked([group_sum, group_sq], 8)
    near_ref[W:, :] = stacked(pieces_of(group_sum) + pieces_of(group_sq), 16).astype(bf16)
    odd = flags_ref[0, 2] > 0.5
    top = x_ref[0:W, :]
    bottom = x_ref[CELLS - W :, :]
    near_ref[0:W, :] = jnp.where(odd, top, bottom)
    far_ref[...] = jnp.where(odd, bottom, top)


def chip_sums_kernel(sums_ref, near_ref, edge_ref, sums_out, far_ref):
    group_sum, group_sq = sums_of(near_ref[W:, :].astype(f32))
    group_sum = group_sum + sums_ref[0:1]
    group_sq = group_sq + sums_ref[1:2]
    sums_out[...] = stacked([group_sum, group_sq], 8)
    far_ref[0:W, :] = edge_ref[...]
    far_ref[W:, :] = stacked(pieces_of(group_sum) + pieces_of(group_sq), 16).astype(bf16)


def reference_kv(weight, states):
    normed = layer_norm(states.astype(f32), None).astype(bf16)
    return dot_t(normed, weight[...]).astype(bf16)


def reference_kernel(
    flags_ref, states_ref, before_ref, key_ref, value_ref, out_ref, half_ref, weight
):
    weight[0:INNER, :] = key_ref[...]
    weight[INNER:, :] = value_ref[...]
    out_ref[...] = reference_kv(weight, states_ref[...])
    half_ref[...] = jnp.where(flags_ref[0, 3] > 0.5, out_ref[PART:, :], out_ref[0:PART, :])


def parts_kernel(first_ref, second_ref, before_ref, *part_refs):
    for i, part_ref in enumerate(part_refs):
        ref = (first_ref, second_ref)[i // 2]
        size = part_ref.shape[0]
        part_ref[...] = ref[i % 2 * size : (i % 2 + 1) * size, :]


def joined_weights(weight, key_ref, value_ref, query_ref):
    weight[0:INNER, :] = key_ref[...]
    weight[INNER:C, :] = value_ref[...]
    weight[C:, :] = query_ref[...]


def conv_kernel(
    flags_ref,
    sums_ref,
    x_ref,
    near_ref,
    far_ref,
    gain_ref,
    kernel_ref,
    norm_gain_ref,
    query_ref,
    key_ref,
    value_ref,
    hidden_out,
    query_out,
    kv_out,
    low_out,
    high_out,
    first_out,
    second_out,
    lhs,
    weight,
):
    joined_weights(weight, key_ref, value_ref, query_ref)
    group_sum, group_sq = sums_of(far_ref[W:, :].astype(f32))
    members = float(4 * CELLS * (C // GROUPS))
    average = (group_sum + sums_ref[0:1]) / members
    variance = (group_sq + sums_ref[1:2]) / members - average * average
    factor = lax.rsqrt(variance + epsilon) * gain_ref[...].reshape(1, C)
    at = lax.broadcasted_iota(jnp.int32, (W, 1), 0)
    odd = flags_ref[0, 2] > 0.5

    def place(r, block, keep):
        v = (block.astype(f32) - average) * factor
        act = (0.5 * v) * (1.0 + jnp.tanh(0.5 * v))
        if keep is not None:
            act = jnp.where(keep > 0.5, act, 0.0)
        rows = slice(r * W, (r + 1) * W)
        lhs[rows, C : 2 * C] = act.astype(bf16)
        lhs[rows, 0:C] = jnp.where(at == 0, 0.0, pltpu.roll(act, 1, 0)).astype(bf16)
        lhs[rows, 2 * C :] = jnp.where(at == W - 1, 0.0, pltpu.roll(act, W - 1, 0)).astype(bf16)

    near, far = near_ref[0:W, :], far_ref[0:W, :]
    place(0, jnp.where(odd, near, far), flags_ref[0, 0])
    place(STRIP + 1, jnp.where(odd, far, near), flags_ref[0, 1])
    for r in range(STRIP):
        place(r + 1, x_ref[r * W : (r + 1) * W, :], None)
    for first in (0, CELLS // 2):
        rows = slice(first, first + CELLS // 2)
        total = None
        for a in range(3):
            part = dot(lhs[first + a * W : first + a * W + CELLS // 2, :], kernel_ref[a])
            total = part if total is None else total + part
        hidden_out[rows, :] = (x_ref[rows, :].astype(f32) + total).astype(bf16)
    normed = layer_norm(hidden_out[...].astype(f32), norm_gain_ref[...].reshape(1, C)).astype(bf16)
    projected = dot_t(normed, weight[...])
    kv = projected[:, 0:C].astype(bf16)
    kv_out[...] = kv
    low_out[...] = kv[0:PART]
    high_out[...] = kv[PART:]
    first_out[...] = kv[0:FIRST]
    second_out[...] = kv[FIRST:]
    query_out[:, 0:INNER] = (projected[:, C:] * QUERY_SCALE).astype(bf16)
    query_out[:, INNER:] = jnp.zeros((CELLS, 64), bf16)


def head_query(query, h):
    low, high = KEY_WINDOW[h]
    lane = lane_iota(high - low, low)
    inside = (lane >= h * HEAD_DIM) & (lane < (h + 1) * HEAD_DIM)
    return jnp.where(inside, query[:, low:high], jnp.zeros((), bf16))


def inside_value(h):
    low, high = VALUE_WINDOW[h]
    lane = lane_iota(high - low, low)
    return (lane >= INNER + h * HEAD_DIM) & (lane < INNER + (h + 1) * HEAD_DIM)


def tiles_of(kv_refs, ranges, scratch):
    tiles = []
    at = 0
    for ref, (low, high) in zip(kv_refs, ranges):
        whole = (high - low) // WHOLE * WHOLE
        if whole == 2 * WHOLE or whole == high - low:
            tiles.append((ref, low, low + whole))
            low += whole
        if low < high:
            scratch[at : at + high - low, :] = ref[low:high, :]
            at += high - low
    return tiles + [(scratch, low, min(low + TILE, at)) for low in range(0, at, TILE)]


def attend(query, tiles, start):
    gathered = []
    for h in range(HEADS):
        key_low, key_high = KEY_WINDOW[h]
        low, high = VALUE_WINDOW[h]
        mine = head_query(query, h)
        inside = inside_value(h)
        acc = None if start is None else start(h)
        for ref, first, last in tiles:
            weights = jnp.exp2(dot_t(mine, ref[first:last, key_low:key_high])).astype(bf16)
            values = jnp.where(inside, ref[first:last, low:high], jnp.ones((), bf16))
            part = dot(weights, values)
            acc = part if acc is None else acc + part
        gathered.append(acc)
    return gathered


def normalised(gathered):
    blocks = [None, None, None]
    for h in range(HEADS):
        low, high = VALUE_WINDOW[h]
        acc = gathered[h]
        spare = 0 if INNER + h * HEAD_DIM > low else high - low - 1
        result = acc * (1.0 / acc[:, spare : spare + 1])
        result = jnp.where(inside_value(h), result, 0.0)
        for b in range((high - low) // LANES):
            at = low // LANES + b - 2
            piece = result[:, b * LANES : (b + 1) * LANES]
            blocks[at] = piece if blocks[at] is None else blocks[at] + piece
    return blocks


def starting(acc_ref):
    return lambda h: acc_ref[:, ACC_AT[h] : ACC_AT[h] + VALUE_WINDOW[h][1] - VALUE_WINDOW[h][0]]


def attention_kernel(ranges, has_start, *refs):
    n_kv = len(ranges)
    query_ref = refs[0]
    start = starting(refs[1 + n_kv]) if has_start else None
    out_ref, scratch = refs[-2:]
    tiles = tiles_of(refs[1 : 1 + n_kv], ranges, scratch)
    for h, acc in enumerate(attend(query_ref[...], tiles, start)):
        out_ref[:, ACC_AT[h] : ACC_AT[h] + acc.shape[1]] = acc


def last_attention_kernel(
    query_ref,
    acc_ref,
    kv_ref,
    hidden_ref,
    weight_ref,
    gain_ref,
    mixed_out,
    sent_out,
    rows,
    weight,
):
    weight[0:64, :] = jnp.zeros((64, C), bf16)
    weight[64:, :] = weight_ref[...]
    blocks = normalised(attend(query_ref[...], [(kv_ref, 0, kv_ref.shape[0])], starting(acc_ref)))
    attended = jnp.concatenate([block.astype(bf16) for block in blocks], axis=1)
    update = dot(attended, weight[...])
    mixed = (hidden_ref[...].astype(f32) + update).astype(bf16)
    mixed_out[...] = mixed
    framed = layer_norm(mixed.astype(f32), gain_ref[...].reshape(1, C))
    for j in range(PLACES):
        for c in range(C // LANES):
            rows[pl.ds(j * 5 + c, FRAMES, stride=SENT + 1), :] = framed[
                j * FRAMES : (j + 1) * FRAMES, c * LANES : (c + 1) * LANES
            ]
    for r in range(PLACES * 5, SENT):
        rows[pl.ds(r, FRAMES, stride=SENT + 1), :] = jnp.zeros((FRAMES, LANES), f32)
    for g in range(FRAMES):
        sent_out[g * SENT : (g + 1) * SENT, :] = rows[
            g * (SENT + 1) : g * (SENT + 1) + SENT, :
        ].astype(bf16)


def temporal_kernel(
    got_ref, query_ref, key_ref, value_ref, out_ref, rows, tokens, result, weight
):
    joined_weights(weight, key_ref, value_ref, query_ref)
    for g in range(FRAMES):
        rows[g * (SENT + 1) : g * (SENT + 1) + SENT, :] = got_ref[
            g * SENT : (g + 1) * SENT, :
        ].astype(f32)
    for j in range(PLACES):
        for c in range(C // LANES):
            tokens[j * FRAMES : (j + 1) * FRAMES, c * LANES : (c + 1) * LANES] = rows[
                pl.ds(j * 5 + c, FRAMES, stride=SENT + 1), :
            ].astype(bf16)
    projected = dot_t(tokens[...], weight[...])
    query = (projected[:, C:] * QUERY_SCALE).astype(bf16)
    query = jnp.concatenate([query, jnp.zeros((CELLS, 64), bf16)], axis=1)
    kv = projected[:, 0:C].astype(bf16)
    span = 3 * FRAMES
    row_place = lax.broadcasted_iota(jnp.int32, (span, span), 0) // FRAMES
    column_place = lax.broadcasted_iota(jnp.int32, (span, span), 1) // FRAMES
    same = row_place == column_place
    for first in range(0, CELLS, span):
        gathered = []
        for h in range(HEADS):
            key_low, key_high = KEY_WINDOW[h]
            low, high = VALUE_WINDOW[h]
            scores = dot_t(
                head_query(query[first : first + span], h),
                kv[first : first + span, key_low:key_high],
            )
            weights = jnp.where(same, jnp.exp2(scores), 0.0).astype(bf16)
            values = jnp.where(
                inside_value(h), kv[first : first + span, low:high], jnp.ones((), bf16)
            )
            gathered.append(dot(weights, values))
        blocks = normalised(gathered)
        for b in range(3):
            result[first : first + span, b * LANES : (b + 1) * LANES] = blocks[b]
    for j in range(PLACES):
        cell = slice(j * FRAMES, (j + 1) * FRAMES)
        for b in range(2):
            rows[pl.ds(j * 2 + b, FRAMES, stride=BACK + 1), :] = result[
                cell, (1 + b) * LANES : (2 + b) * LANES
            ]
    for pair in range((PLACES + 1) // 2):
        half = result[2 * pair * FRAMES : (2 * pair + 1) * FRAMES, 0:LANES]
        if 2 * pair + 1 < PLACES:
            other = result[(2 * pair + 1) * FRAMES : (2 * pair + 2) * FRAMES, 0:LANES]
            half = half + pltpu.roll(other, LANES // 2, 1)
        rows[pl.ds(2 * PLACES + pair, FRAMES, stride=BACK + 1), :] = half
    rows[pl.ds(BACK - 1, FRAMES, stride=BACK + 1), :] = jnp.zeros((FRAMES, LANES), f32)
    for g in range(0, FRAMES, 2):
        pair = [rows[i * (BACK + 1) : i * (BACK + 1) + BACK, :] for i in (g, g + 1)]
        out_ref[g * BACK : (g + 2) * BACK, :] = jnp.concatenate(pair, axis=0).astype(bf16)


def final_kernel(got_ref, weight_ref, mixed_ref, out_ref, rows, attended, weight, staged, left):
    weight[0:64, :] = jnp.zeros((64, C), bf16)
    weight[64:, :] = weight_ref[...]
    for g in range(0, FRAMES, 2):
        pair = got_ref[g * BACK : (g + 2) * BACK, :].astype(f32)
        for i in range(2):
            rows[(g + i) * (BACK + 1) : (g + i) * (BACK + 1) + BACK, :] = pair[
                i * BACK : (i + 1) * BACK, :
            ]
    upper = lane_iota(LANES) >= LANES // 2
    parts = 3
    copies = []
    for part in range(parts):
        for j in range(part * PLACES // parts, (part + 1) * PLACES // parts):
            cell = slice(j * FRAMES, (j + 1) * FRAMES)
            for b in range(2):
                attended[cell, (1 + b) * LANES : (2 + b) * LANES] = rows[
                    pl.ds(j * 2 + b, FRAMES, stride=BACK + 1), :
                ].astype(bf16)
            half = rows[pl.ds(2 * PLACES + j // 2, FRAMES, stride=BACK + 1), :]
            if j % 2:
                half = pltpu.roll(half, LANES // 2, 1)
            attended[cell, 0:LANES] = jnp.where(upper, half, 0.0).astype(bf16)
        size = CELLS // parts
        cells = slice(part * size, (part + 1) * size)
        update = dot(attended[cells, :], weight[...])
        staged[cells, :] = (mixed_ref[cells, :].astype(f32) + update).astype(bf16)
        at = pl.ds(part * size, size)
        copies.append(pltpu.make_async_copy(staged.at[at], out_ref.at[at], left.at[part]))
        copies[-1].start()
    for copy in copies:
        copy.wait()


def order_kernel(value_ref, before_ref, out_ref):
    pass


def after(value, before):
    return pl.pallas_call(
        order_kernel,
        out_shape=struct(value.shape, value.dtype),
        in_specs=[pl.BlockSpec(memory_space=pl.ANY)] * 2,
        out_specs=pl.BlockSpec(memory_space=pl.ANY),
        input_output_aliases={0: 0},
        compiler_params=pltpu.CompilerParams(vmem_limit_bytes=1 << 20),
        cost_estimate=pl.CostEstimate(flops=0, bytes_accessed=0, transcendentals=0),
    )(value, before)


def struct(shape, dtype):
    return jax.ShapeDtypeStruct(shape, dtype)


def on_device(
    latent,
    reference_states,
    group_gain,
    conv_weight,
    norm_gain,
    spatial_query,
    spatial_key,
    spatial_value,
    spatial_out,
    frame_gain,
    temporal_query,
    temporal_key,
    temporal_value,
    temporal_out,
):
    x = latent.reshape(CELLS, C)
    strip_at = lax.axis_index("space")
    odd_row = lax.axis_index("frame") // 8 % 2 == 1
    flags = (
        jnp.stack([strip_at > 0, strip_at < 3, strip_at % 2 == 1, odd_row])
        .astype(f32)
        .reshape(1, 4)
    )

    def swap(value, k):
        return lax.ppermute(value, "space", [(i, i ^ k) for i in range(4)])

    states = reference_states.reshape(CELLS, C)
    sums, near, edge = call(
        stats_kernel,
        [struct((8, C), f32), struct((W + 16, C), bf16), struct((W, C), bf16)],
        [flags, x],
        smem=1,
        flops=2 * 10**9,
    )
    near = swap(near, 1)
    sums, far = call(
        chip_sums_kernel,
        [struct((8, C), f32), struct((W + 16, C), bf16)],
        [sums, near, edge],
        flops=2 * 10**9,
    )
    far = swap(far, 3)

    ref_kv, half = call(
        reference_kernel,
        [struct((CELLS, C), bf16), struct((CELLS // 2, C), bf16)],
        [flags, states, sums, spatial_key.T, spatial_value.T],
        scratch=[pltpu.VMEM((C, C), bf16)],
        smem=1,
        flops=2 * 10**9,
        limit=8,
    )
    half = swap(half, 2)

    hidden, query, kv, low, high, first, second = call(
        conv_kernel,
        [
            struct((CELLS, C), bf16),
            struct((CELLS, 384), bf16),
            struct((CELLS, C), bf16),
            struct((PART, C), bf16),
            struct((PART, C), bf16),
            struct((FIRST, C), bf16),
            struct((CELLS - FIRST, C), bf16),
        ],
        [
            flags,
            sums,
            x,
            near,
            far,
            group_gain,
            conv_weight.reshape(3, 3 * C, C),
            norm_gain,
            spatial_query.T,
            spatial_key.T,
            spatial_value.T,
        ],
        scratch=[
            pltpu.VMEM(((STRIP + 2) * W, 3 * C), bf16),
            pltpu.VMEM((C + INNER, C), bf16),
        ],
        smem=1,
        limit=16,
    )

    ref_near = swap(ref_kv, 1)
    half = after(half, query)
    other_half = lax.ppermute(half, "frame", [(f, f ^ 8) for f in range(FRAMES)])
    half_near = swap(half, 1)
    first = swap(first, 2)
    second = swap(second, 2)
    kv_near = [swap(low, 1), swap(high, 1)]

    def attention(kv_parts, start):
        ranges = [(low, high) for _, low, high in kv_parts]
        keys = sum(high - low for low, high in ranges)
        return call(
            functools.partial(attention_kernel, ranges, start is not None),
            struct((CELLS, ACC_WIDTH), f32),
            [query, *(part for part, _, _ in kv_parts)] + ([] if start is None else [start]),
            scratch=[pltpu.VMEM((keys, C), bf16)],
            limit=16,
        )

    acc = attention(
        [(part, 0, part.shape[0]) for part in (kv, *kv_near, ref_kv, ref_near, half)]
        + [(half_near, 0, EARLY)],
        None,
    )
    sizes = (PART // 2, PART // 2, FIRST // 2, FIRST // 2)
    parts = call(
        parts_kernel,
        [struct((size, C), bf16) for size in sizes],
        [other_half, first, acc],
        anywhere=(2,),
    )
    near_parts = [swap(part, 1) for part in parts]
    acc = attention(
        [(half_near, EARLY, PART), (parts[0], 0, PART // 2), (parts[1], 0, HEAD)], acc
    )
    rest = [parts[1], *near_parts[:2], *parts[2:], *near_parts[2:]]
    acc = attention([(part, HEAD if i == 0 else 0, part.shape[0]) for i, part in enumerate(rest)], acc)
    second = after(second, acc)
    second_near = swap(second, 1)
    acc = attention([(second, 0, CELLS - FIRST)], acc)
    mixed, sent = call(
        last_attention_kernel,
        [struct((CELLS, C), bf16), struct((FRAMES * SENT, LANES), bf16)],
        [query, acc, second_near, hidden, spatial_out, frame_gain],
        scratch=[
            pltpu.VMEM((FRAMES * (SENT + 1), LANES), f32),
            pltpu.VMEM((384, C), bf16),
        ],
        limit=16,
    )
    got = lax.all_to_all(
        sent.reshape(FRAMES, SENT, LANES), "frame", split_axis=0, concat_axis=0, axis_index_groups=[ORDER], tiled=True
    )
    back = call(
        temporal_kernel,
        struct((FRAMES * BACK, LANES), bf16),
        [
            got.reshape(FRAMES * SENT, LANES),
            temporal_query.T,
            temporal_key.T,
            temporal_value.T,
        ],
        scratch=[
            pltpu.VMEM((FRAMES * (SENT + 1), LANES), f32),
            pltpu.VMEM((CELLS, C), bf16),
            pltpu.VMEM((CELLS, 384), f32),
            pltpu.VMEM((C + INNER, C), bf16),
        ],
    )
    returned = lax.all_to_all(
        back.reshape(FRAMES, BACK, LANES), "frame", split_axis=0, concat_axis=0, axis_index_groups=[ORDER], tiled=True
    )
    output = call(
        final_kernel,
        struct((CELLS, C), bf16),
        [returned.reshape(FRAMES * BACK, LANES), temporal_out, mixed],
        scratch=[
            pltpu.VMEM((FRAMES * (BACK + 1), LANES), f32),
            pltpu.VMEM((CELLS, 384), bf16),
            pltpu.VMEM((384, C), bf16),
            pltpu.VMEM((CELLS, C), bf16),
            pltpu.SemaphoreType.DMA((3,)),
        ],
        out_anywhere=True,
    )
    return output.reshape(latent.shape)


def solution(mesh):
    return jax.shard_map(
        on_device,
        mesh=mesh,
        in_specs=(P("frame", "space", None, None), P("space", None, None)) + (P(),) * 12,
        out_specs=P("frame", "space", None, None),
        check_vma=False,
    )
```

```python
import functools

import jax
import jax.numpy as jnp
from jax import lax
from jax.experimental import pallas as pl
from jax.experimental.pallas import tpu as pltpu
from jax.sharding import PartitionSpec as P

HEADS = 4
HEAD_DIM = 80
GROUPS = 32
INNER = 320
C = 640
W = 48
STRIP = 12
CELLS = STRIP * W
FRAMES = 64
PLACES = CELLS // FRAMES
LANES = 128
SENT = 48
WHOLE = 256
TILE = 768
EARLY = 224
HEAD = 48
FIRST = 320
PART = CELLS // 2
BACK = 24

epsilon = 1e-05
QUERY_SCALE = HEAD_DIM**-0.5 * 1.4426950408889634

KEY_WINDOW = ((0, 128), (0, 256), (128, 256), (128, 384))
VALUE_WINDOW = ((256, 512), (384, 512), (384, 640), (512, 640))
ACC_AT = (0, 256, 384, 640)
ACC_WIDTH = 768

ORDER = [(x * 4 + y) * 8 + z for z in range(8) for y in range(4) for x in range(2)]

f32 = jnp.float32
bf16 = jnp.bfloat16


def lane_iota(width, start=0):
    return lax.broadcasted_iota(jnp.int32, (1, width), 1) + start


def layer_norm(values, factor):
    centre = jnp.mean(values, axis=-1, keepdims=True)
    shifted = values - centre
    spread = jnp.mean(shifted * shifted, axis=-1, keepdims=True)
    normed = shifted * lax.rsqrt(spread + epsilon)
    return normed if factor is None else normed * factor


def dot(a, b):
    return jnp.dot(a, b, preferred_element_type=f32)


def dot_t(a, b):
    return lax.dot_general(a, b, (((1,), (1,)), ((), ())), preferred_element_type=f32)


def vmem(count):
    return [pl.BlockSpec(memory_space=pltpu.VMEM)] * count


def call(
    body, outs, operands, scratch=(), smem=0, limit=8, anywhere=(), flops=0, out_anywhere=False
):
    single = not isinstance(outs, (list, tuple))
    specs = [pl.BlockSpec(memory_space=pltpu.SMEM)] * smem + vmem(len(operands) - smem)
    for i in anywhere:
        specs[i] = pl.BlockSpec(memory_space=pl.ANY)
    return pl.pallas_call(
        body,
        out_shape=outs,
        in_specs=specs,
        out_specs=pl.BlockSpec(memory_space=pl.ANY)
        if out_anywhere
        else vmem(1)[0]
        if single
        else vmem(len(outs)),
        scratch_shapes=list(scratch),
        compiler_params=pltpu.CompilerParams(vmem_limit_bytes=limit * 1024 * 1024),
        cost_estimate=pl.CostEstimate(flops=flops, bytes_accessed=0, transcendentals=0),
    )(*operands)


def pieces_of(value):
    high = value.astype(bf16).astype(f32)
    middle = (value - high).astype(bf16).astype(f32)
    return [high, middle, value - high - middle]


def stacked(rows, height):
    at = lax.broadcasted_iota(jnp.int32, (height, C), 0)
    result = jnp.zeros((height, C), f32)
    for i, row in enumerate(rows):
        result = jnp.where(at == i, row, result)
    return result


def sums_of(pieces):
    return pieces[0:1] + pieces[1:2] + pieces[2:3], pieces[3:4] + pieces[4:5] + pieces[5:6]


def stats_kernel(flags_ref, x_ref, sums_ref, near_ref, far_ref):
    total = jnp.zeros((1, C), f32)
    square = jnp.zeros((1, C), f32)
    for r in range(STRIP):
        v = x_ref[r * W : (r + 1) * W, :].astype(f32)
        total = total + jnp.sum(v, axis=0, keepdims=True)
        square = square + jnp.sum(v * v, axis=0, keepdims=True)
    per = C // GROUPS
    column_group = jnp.floor((lane_iota(C).astype(f32) + 0.5) * (1.0 / per))
    row_at = lax.broadcasted_iota(jnp.int32, (C, 1), 0).astype(f32)
    row_group = jnp.floor((row_at + 0.5) * (1.0 / per))
    same = jnp.where(row_group == column_group, 1.0, 0.0).astype(bf16)
    grouped = dot(stacked(pieces_of(total) + pieces_of(square), 16).astype(bf16), same)
    group_sum, group_sq = sums_of(grouped)
    sums_ref[...] = stacked([group_sum, group_sq], 8)
    near_ref[W:, :] = stacked(pieces_of(group_sum) + pieces_of(group_sq), 16).astype(bf16)
    odd = flags_ref[0, 2] > 0.5
    top = x_ref[0:W, :]
    bottom = x_ref[CELLS - W :, :]
    near_ref[0:W, :] = jnp.where(odd, top, bottom)
    far_ref[...] = jnp.where(odd, bottom, top)


def chip_sums_kernel(sums_ref, near_ref, edge_ref, sums_out, far_ref):
    group_sum, group_sq = sums_of(near_ref[W:, :].astype(f32))
    group_sum = group_sum + sums_ref[0:1]
    group_sq = group_sq + sums_ref[1:2]
    sums_out[...] = stacked([group_sum, group_sq], 8)
    far_ref[0:W, :] = edge_ref[...]
    far_ref[W:, :] = stacked(pieces_of(group_sum) + pieces_of(group_sq), 16).astype(bf16)


def reference_kv(weight, states):
    normed = layer_norm(states.astype(f32), None).astype(bf16)
    return dot_t(normed, weight[...]).astype(bf16)


def reference_kernel(
    flags_ref, states_ref, before_ref, key_ref, value_ref, query_ref, out_ref, half_ref, weight
):
    joined_weights(weight, key_ref, value_ref, query_ref)
    out_ref[...] = reference_kv(weight.at[0:C], states_ref[...])
    half_ref[...] = jnp.where(flags_ref[0, 3] > 0.5, out_ref[PART:, :], out_ref[0:PART, :])


def parts_kernel(first_ref, second_ref, before_ref, *part_refs):
    for i, part_ref in enumerate(part_refs):
        ref = (first_ref, second_ref)[i // 2]
        size = part_ref.shape[0]
        part_ref[...] = ref[i % 2 * size : (i % 2 + 1) * size, :]


def joined_weights(weight, key_ref, value_ref, query_ref):
    weight[0:INNER, :] = key_ref[...]
    weight[INNER:C, :] = value_ref[...]
    weight[C:, :] = query_ref[...]


def conv_kernel(
    flags_ref,
    sums_ref,
    x_ref,
    near_ref,
    far_ref,
    gain_ref,
    kernel_ref,
    norm_gain_ref,
    weight,
    hidden_out,
    query_out,
    kv_out,
    low_out,
    high_out,
    first_out,
    second_out,
    lhs,
):
    group_sum, group_sq = sums_of(far_ref[W:, :].astype(f32))
    members = float(4 * CELLS * (C // GROUPS))
    average = (group_sum + sums_ref[0:1]) / members
    variance = (group_sq + sums_ref[1:2]) / members - average * average
    factor = lax.rsqrt(variance + epsilon) * gain_ref[...].reshape(1, C)
    at = lax.broadcasted_iota(jnp.int32, (W, 1), 0)
    odd = flags_ref[0, 2] > 0.5

    def place(r, block, keep):
        v = (block.astype(f32) - average) * factor
        act = (0.5 * v) * (1.0 + jnp.tanh(0.5 * v))
        if keep is not None:
            act = jnp.where(keep > 0.5, act, 0.0)
        rows = slice(r * W, (r + 1) * W)
        lhs[rows, C : 2 * C] = act.astype(bf16)
        lhs[rows, 0:C] = jnp.where(at == 0, 0.0, pltpu.roll(act, 1, 0)).astype(bf16)
        lhs[rows, 2 * C :] = jnp.where(at == W - 1, 0.0, pltpu.roll(act, W - 1, 0)).astype(bf16)

    near, far = near_ref[0:W, :], far_ref[0:W, :]
    place(0, jnp.where(odd, near, far), flags_ref[0, 0])
    place(STRIP + 1, jnp.where(odd, far, near), flags_ref[0, 1])
    for r in range(STRIP):
        place(r + 1, x_ref[r * W : (r + 1) * W, :], None)
    for first in (0, CELLS // 2):
        rows = slice(first, first + CELLS // 2)
        total = None
        for a in range(3):
            part = dot(lhs[first + a * W : first + a * W + CELLS // 2, :], kernel_ref[a])
            total = part if total is None else total + part
        hidden_out[rows, :] = (x_ref[rows, :].astype(f32) + total).astype(bf16)
    normed = layer_norm(hidden_out[...].astype(f32), norm_gain_ref[...].reshape(1, C)).astype(bf16)
    projected = dot_t(normed, weight[...])
    kv = projected[:, 0:C].astype(bf16)
    kv_out[...] = kv
    low_out[...] = kv[0:PART]
    high_out[...] = kv[PART:]
    first_out[...] = kv[0:FIRST]
    second_out[...] = kv[FIRST:]
    query_out[:, 0:INNER] = (projected[:, C:] * QUERY_SCALE).astype(bf16)
    query_out[:, INNER:] = jnp.zeros((CELLS, 64), bf16)


def head_query(query, h):
    low, high = KEY_WINDOW[h]
    lane = lane_iota(high - low, low)
    inside = (lane >= h * HEAD_DIM) & (lane < (h + 1) * HEAD_DIM)
    return jnp.where(inside, query[:, low:high], jnp.zeros((), bf16))


def inside_value(h):
    low, high = VALUE_WINDOW[h]
    lane = lane_iota(high - low, low)
    return (lane >= INNER + h * HEAD_DIM) & (lane < INNER + (h + 1) * HEAD_DIM)


def tiles_of(kv_refs, ranges, scratch):
    tiles = []
    at = 0
    for ref, (low, high) in zip(kv_refs, ranges):
        whole = (high - low) // WHOLE * WHOLE
        if whole == 2 * WHOLE or whole == high - low:
            tiles.append((ref, low, low + whole))
            low += whole
        if low < high:
            scratch[at : at + high - low, :] = ref[low:high, :]
            at += high - low
    return tiles + [(scratch, low, min(low + TILE, at)) for low in range(0, at, TILE)]


def attend(query, tiles, start):
    gathered = []
    for h in range(HEADS):
        key_low, key_high = KEY_WINDOW[h]
        low, high = VALUE_WINDOW[h]
        mine = head_query(query, h)
        inside = inside_value(h)
        acc = None if start is None else start(h)
        for ref, first, last in tiles:
            weights = jnp.exp2(dot_t(mine, ref[first:last, key_low:key_high])).astype(bf16)
            values = jnp.where(inside, ref[first:last, low:high], jnp.ones((), bf16))
            part = dot(weights, values)
            acc = part if acc is None else acc + part
        gathered.append(acc)
    return gathered


def normalised(gathered):
    blocks = [None, None, None]
    for h in range(HEADS):
        low, high = VALUE_WINDOW[h]
        acc = gathered[h]
        spare = 0 if INNER + h * HEAD_DIM > low else high - low - 1
        result = acc * (1.0 / acc[:, spare : spare + 1])
        result = jnp.where(inside_value(h), result, 0.0)
        for b in range((high - low) // LANES):
            at = low // LANES + b - 2
            piece = result[:, b * LANES : (b + 1) * LANES]
            blocks[at] = piece if blocks[at] is None else blocks[at] + piece
    return blocks


def starting(acc_ref):
    return lambda h: acc_ref[:, ACC_AT[h] : ACC_AT[h] + VALUE_WINDOW[h][1] - VALUE_WINDOW[h][0]]


def attention_kernel(ranges, has_start, *refs):
    n_kv = len(ranges)
    query_ref = refs[0]
    start = starting(refs[1 + n_kv]) if has_start else None
    out_ref, scratch = refs[-2:]
    tiles = tiles_of(refs[1 : 1 + n_kv], ranges, scratch)
    for h, acc in enumerate(attend(query_ref[...], tiles, start)):
        out_ref[:, ACC_AT[h] : ACC_AT[h] + acc.shape[1]] = acc


def last_attention_kernel(
    query_ref,
    acc_ref,
    kv_ref,
    hidden_ref,
    weight_ref,
    gain_ref,
    mixed_out,
    sent_out,
    rows,
    weight,
):
    weight[0:64, :] = jnp.zeros((64, C), bf16)
    weight[64:, :] = weight_ref[...]
    blocks = normalised(attend(query_ref[...], [(kv_ref, 0, kv_ref.shape[0])], starting(acc_ref)))
    attended = jnp.concatenate([block.astype(bf16) for block in blocks], axis=1)
    update = dot(attended, weight[...])
    mixed = (hidden_ref[...].astype(f32) + update).astype(bf16)
    mixed_out[...] = mixed
    framed = layer_norm(mixed.astype(f32), gain_ref[...].reshape(1, C))
    for j in range(PLACES):
        for c in range(C // LANES):
            rows[pl.ds(j * 5 + c, FRAMES, stride=SENT + 1), :] = framed[
                j * FRAMES : (j + 1) * FRAMES, c * LANES : (c + 1) * LANES
            ]
    for r in range(PLACES * 5, SENT):
        rows[pl.ds(r, FRAMES, stride=SENT + 1), :] = jnp.zeros((FRAMES, LANES), f32)
    for g in range(FRAMES):
        sent_out[g * SENT : (g + 1) * SENT, :] = rows[
            g * (SENT + 1) : g * (SENT + 1) + SENT, :
        ].astype(bf16)


def temporal_kernel(
    got_ref, query_ref, key_ref, value_ref, out_ref, rows, tokens, result, weight
):
    joined_weights(weight, key_ref, value_ref, query_ref)
    for g in range(FRAMES):
        rows[g * (SENT + 1) : g * (SENT + 1) + SENT, :] = got_ref[
            g * SENT : (g + 1) * SENT, :
        ].astype(f32)
    for j in range(PLACES):
        for c in range(C // LANES):
            tokens[j * FRAMES : (j + 1) * FRAMES, c * LANES : (c + 1) * LANES] = rows[
                pl.ds(j * 5 + c, FRAMES, stride=SENT + 1), :
            ].astype(bf16)
    projected = dot_t(tokens[...], weight[...])
    query = (projected[:, C:] * QUERY_SCALE).astype(bf16)
    query = jnp.concatenate([query, jnp.zeros((CELLS, 64), bf16)], axis=1)
    kv = projected[:, 0:C].astype(bf16)
    span = 3 * FRAMES
    row_place = lax.broadcasted_iota(jnp.int32, (span, span), 0) // FRAMES
    column_place = lax.broadcasted_iota(jnp.int32, (span, span), 1) // FRAMES
    same = row_place == column_place
    for first in range(0, CELLS, span):
        gathered = []
        for h in range(HEADS):
            key_low, key_high = KEY_WINDOW[h]
            low, high = VALUE_WINDOW[h]
            scores = dot_t(
                head_query(query[first : first + span], h),
                kv[first : first + span, key_low:key_high],
            )
            weights = jnp.where(same, jnp.exp2(scores), 0.0).astype(bf16)
            values = jnp.where(
                inside_value(h), kv[first : first + span, low:high], jnp.ones((), bf16)
            )
            gathered.append(dot(weights, values))
        blocks = normalised(gathered)
        for b in range(3):
            result[first : first + span, b * LANES : (b + 1) * LANES] = blocks[b]
    for j in range(PLACES):
        cell = slice(j * FRAMES, (j + 1) * FRAMES)
        for b in range(2):
            rows[pl.ds(j * 2 + b, FRAMES, stride=BACK + 1), :] = result[
                cell, (1 + b) * LANES : (2 + b) * LANES
            ]
    for pair in range((PLACES + 1) // 2):
        half = result[2 * pair * FRAMES : (2 * pair + 1) * FRAMES, 0:LANES]
        if 2 * pair + 1 < PLACES:
            other = result[(2 * pair + 1) * FRAMES : (2 * pair + 2) * FRAMES, 0:LANES]
            half = half + pltpu.roll(other, LANES // 2, 1)
        rows[pl.ds(2 * PLACES + pair, FRAMES, stride=BACK + 1), :] = half
    rows[pl.ds(BACK - 1, FRAMES, stride=BACK + 1), :] = jnp.zeros((FRAMES, LANES), f32)
    for g in range(0, FRAMES, 2):
        pair = [rows[i * (BACK + 1) : i * (BACK + 1) + BACK, :] for i in (g, g + 1)]
        out_ref[g * BACK : (g + 2) * BACK, :] = jnp.concatenate(pair, axis=0).astype(bf16)


def final_kernel(got_ref, weight_ref, mixed_ref, out_ref, rows, attended, weight, staged, left):
    weight[0:64, :] = jnp.zeros((64, C), bf16)
    weight[64:, :] = weight_ref[...]
    for g in range(0, FRAMES, 2):
        pair = got_ref[g * BACK : (g + 2) * BACK, :].astype(f32)
        for i in range(2):
            rows[(g + i) * (BACK + 1) : (g + i) * (BACK + 1) + BACK, :] = pair[
                i * BACK : (i + 1) * BACK, :
            ]
    upper = lane_iota(LANES) >= LANES // 2
    parts = 3
    copies = []
    for part in range(parts):
        for j in range(part * PLACES // parts, (part + 1) * PLACES // parts):
            cell = slice(j * FRAMES, (j + 1) * FRAMES)
            for b in range(2):
                attended[cell, (1 + b) * LANES : (2 + b) * LANES] = rows[
                    pl.ds(j * 2 + b, FRAMES, stride=BACK + 1), :
                ].astype(bf16)
            half = rows[pl.ds(2 * PLACES + j // 2, FRAMES, stride=BACK + 1), :]
            if j % 2:
                half = pltpu.roll(half, LANES // 2, 1)
            attended[cell, 0:LANES] = jnp.where(upper, half, 0.0).astype(bf16)
        size = CELLS // parts
        cells = slice(part * size, (part + 1) * size)
        update = dot(attended[cells, :], weight[...])
        staged[cells, :] = (mixed_ref[cells, :].astype(f32) + update).astype(bf16)
        at = pl.ds(part * size, size)
        copies.append(pltpu.make_async_copy(staged.at[at], out_ref.at[at], left.at[part]))
        copies[-1].start()
    for copy in copies:
        copy.wait()


def order_kernel(value_ref, before_ref, out_ref):
    pass


def after(value, before):
    return pl.pallas_call(
        order_kernel,
        out_shape=struct(value.shape, value.dtype),
        in_specs=[pl.BlockSpec(memory_space=pl.ANY)] * 2,
        out_specs=pl.BlockSpec(memory_space=pl.ANY),
        input_output_aliases={0: 0},
        compiler_params=pltpu.CompilerParams(vmem_limit_bytes=1 << 20),
        cost_estimate=pl.CostEstimate(flops=0, bytes_accessed=0, transcendentals=0),
    )(value, before)


def struct(shape, dtype):
    return jax.ShapeDtypeStruct(shape, dtype)


def on_device(
    latent,
    reference_states,
    group_gain,
    conv_weight,
    norm_gain,
    spatial_query,
    spatial_key,
    spatial_value,
    spatial_out,
    frame_gain,
    temporal_query,
    temporal_key,
    temporal_value,
    temporal_out,
):
    x = latent.reshape(CELLS, C)
    strip_at = lax.axis_index("space")
    odd_row = lax.axis_index("frame") // 8 % 2 == 1
    flags = (
        jnp.stack([strip_at > 0, strip_at < 3, strip_at % 2 == 1, odd_row])
        .astype(f32)
        .reshape(1, 4)
    )

    def swap(value, k):
        return lax.ppermute(value, "space", [(i, i ^ k) for i in range(4)])

    states = reference_states.reshape(CELLS, C)
    sums, near, edge = call(
        stats_kernel,
        [struct((8, C), f32), struct((W + 16, C), bf16), struct((W, C), bf16)],
        [flags, x],
        smem=1,
        flops=2 * 10**9,
    )
    near = swap(near, 1)
    sums, far = call(
        chip_sums_kernel,
        [struct((8, C), f32), struct((W + 16, C), bf16)],
        [sums, near, edge],
        flops=2 * 10**9,
    )
    far = swap(far, 3)

    ref_kv, half, weight = call(
        reference_kernel,
        [struct((CELLS, C), bf16), struct((PART, C), bf16), struct((C + INNER, C), bf16)],
        [flags, states, sums, spatial_key.T, spatial_value.T, spatial_query.T],
        smem=1,
        flops=2 * 10**9,
        limit=8,
    )
    half = swap(half, 2)

    hidden, query, kv, low, high, first, second = call(
        conv_kernel,
        [
            struct((CELLS, C), bf16),
            struct((CELLS, 384), bf16),
            struct((CELLS, C), bf16),
            struct((PART, C), bf16),
            struct((PART, C), bf16),
            struct((FIRST, C), bf16),
            struct((CELLS - FIRST, C), bf16),
        ],
        [
            flags,
            sums,
            x,
            near,
            far,
            group_gain,
            conv_weight.reshape(3, 3 * C, C),
            norm_gain,
            weight,
        ],
        scratch=[
            pltpu.VMEM(((STRIP + 2) * W, 3 * C), bf16),
        ],
        smem=1,
        limit=16,
    )

    ref_near = swap(ref_kv, 1)
    half = after(half, query)
    other_half = lax.ppermute(half, "frame", [(f, f ^ 8) for f in range(FRAMES)])
    half_near = swap(half, 1)
    first = swap(first, 2)
    second = swap(second, 2)
    kv_near = [swap(low, 1), swap(high, 1)]

    def attention(kv_parts, start):
        ranges = [(low, high) for _, low, high in kv_parts]
        keys = sum(high - low for low, high in ranges)
        return call(
            functools.partial(attention_kernel, ranges, start is not None),
            struct((CELLS, ACC_WIDTH), f32),
            [query, *(part for part, _, _ in kv_parts)] + ([] if start is None else [start]),
            scratch=[pltpu.VMEM((keys, C), bf16)],
            limit=16,
        )

    acc = attention(
        [(part, 0, part.shape[0]) for part in (kv, *kv_near, ref_kv, ref_near, half)]
        + [(half_near, 0, EARLY)],
        None,
    )
    sizes = (PART // 2, PART // 2, FIRST // 2, FIRST // 2)
    parts = call(
        parts_kernel,
        [struct((size, C), bf16) for size in sizes],
        [other_half, first, acc],
        anywhere=(2,),
    )
    near_parts = [swap(part, 1) for part in parts]
    acc = attention(
        [(half_near, EARLY, PART), (parts[0], 0, PART // 2), (parts[1], 0, HEAD)], acc
    )
    rest = [parts[1], *near_parts[:2], *parts[2:], *near_parts[2:]]
    acc = attention([(part, HEAD if i == 0 else 0, part.shape[0]) for i, part in enumerate(rest)], acc)
    second = after(second, acc)
    second_near = swap(second, 1)
    acc = attention([(second, 0, CELLS - FIRST)], acc)
    mixed, sent = call(
        last_attention_kernel,
        [struct((CELLS, C), bf16), struct((FRAMES * SENT, LANES), bf16)],
        [query, acc, second_near, hidden, spatial_out, frame_gain],
        scratch=[
            pltpu.VMEM((FRAMES * (SENT + 1), LANES), f32),
            pltpu.VMEM((384, C), bf16),
        ],
        limit=16,
    )
    got = lax.all_to_all(
        sent.reshape(FRAMES, SENT, LANES), "frame", split_axis=0, concat_axis=0, axis_index_groups=[ORDER], tiled=True
    )
    back = call(
        temporal_kernel,
        struct((FRAMES * BACK, LANES), bf16),
        [
            got.reshape(FRAMES * SENT, LANES),
            temporal_query.T,
            temporal_key.T,
            temporal_value.T,
        ],
        scratch=[
            pltpu.VMEM((FRAMES * (SENT + 1), LANES), f32),
            pltpu.VMEM((CELLS, C), bf16),
            pltpu.VMEM((CELLS, 384), f32),
            pltpu.VMEM((C + INNER, C), bf16),
        ],
    )
    returned = lax.all_to_all(
        back.reshape(FRAMES, BACK, LANES), "frame", split_axis=0, concat_axis=0, axis_index_groups=[ORDER], tiled=True
    )
    output = call(
        final_kernel,
        struct((CELLS, C), bf16),
        [returned.reshape(FRAMES * BACK, LANES), temporal_out, mixed],
        scratch=[
            pltpu.VMEM((FRAMES * (BACK + 1), LANES), f32),
            pltpu.VMEM((CELLS, 384), bf16),
            pltpu.VMEM((384, C), bf16),
            pltpu.VMEM((CELLS, C), bf16),
            pltpu.SemaphoreType.DMA((3,)),
        ],
        out_anywhere=True,
    )
    return output.reshape(latent.shape)


def solution(mesh):
    return jax.shard_map(
        on_device,
        mesh=mesh,
        in_specs=(P("frame", "space", None, None), P("space", None, None)) + (P(),) * 12,
        out_specs=P("frame", "space", None, None),
        check_vma=False,
    )
```
